512 devices in a mesh: tgt: 32 (over y, z_hi), src: 16 (over x, z_lo, core).
Axes of the slice: x: 4, y: 8, z: 8 (z_hi: 4, z_lo: 2; z = z_hi * 2 + z_lo), core: 2. Of those that a mesh axis runs over, the one named last changes fastest.
Arguments:
- lattice: int32 [2, 16384], P(None, ('tgt', 'src')), may hold values from 0 to 255, as said below
- material: int32 [16384], P(('tgt', 'src')), may hold values from 0 to 15
- polarizability: float32 [4, 16, 4], replicated, may hold values from -1.2 to 1.2
- wavenumber: float32 [4], replicated, may hold values from 2 to 3.5
- dipoles: bfloat16 [4, 2, 6, 4, 16384], P(None, None, None, None, ('tgt', 'src')), may hold values from -6 to 6
- adjoint_in: bfloat16 [4, 2, 6, 4, 16384], P(None, None, None, None, ('tgt', 'src')), may hold values from -6 to 6
Outputs:
- forward_out: float32 [4, 2, 6, 4, 16384], P(None, None, None, None, ('tgt', 'src'))
- adjoint_out: float32 [4, 2, 6, 4, 16384], P(None, None, None, None, ('tgt', 'src'))
The draws below stay inside these ranges and needn't reach their ends.
Inputs may be any that keep to these rules, and one draw needn't show every extreme that they name: Atoms are numbered tile by tile, the second tile index fastest; a tile spans 2 x 16 lattice sites, and its 32 atoms occupy each of its sites exactly once, in any order. The first index runs from 0 to 63, the second from 0 to 255.
All inputs are finite; a program needn't handle non-finite values.
Results may differ from the reference program's by a relative error of at most 0.0039.
Values may be sent and summed in bfloat16 or wider, within the bound.
A program may use at most 64 MiB of HBM per device.

```python
import math
import jax
import jax.numpy as jnp
from jax import lax

WAVES = 4
EXCITE = 4
TYPES = 16
TILE_Y = 16
TILE_X = 2
ATOMS = 32
LATTICE_X = 64
LATTICE_Y = 256
ATOMS_ALL = 16384
N_TGT = 32
N_SRC = 16


def draw_lattice(key, part):
    columns = LATTICE_Y // TILE_Y
    blocks = LATTICE_X // TILE_X * columns
    subkeys = jax.random.split(jax.random.fold_in(key, 11), blocks)
    placed = jax.vmap(lambda subkey: jax.random.permutation(subkey, ATOMS))(subkeys).astype(jnp.int32)
    block_id = jnp.arange(blocks, dtype=jnp.int32)[:, None]
    first = block_id // columns * TILE_X + placed // TILE_Y
    second = block_id % columns * TILE_Y + placed % TILE_Y
    return jnp.stack([first.reshape(-1), second.reshape(-1)]).astype(jnp.int32)


def with_ends(values, own_key, smallest, top_value):
    longest = values.shape.index(max(values.shape))
    spots = []
    for shift in (0, 1):
        where = [jax.random.randint(jax.random.fold_in(own_key, axis), (), 0, length) for axis, length in enumerate(values.shape)]
        where[longest] = (where[longest] + shift) % values.shape[longest]
        spots.append(tuple(where))
    return values.at[spots[0]].set(smallest).at[spots[1]].set(top_value)


def block_scale(own_key, extent, cuts, least, high):
    factor_of = 1.0
    for dim, shards_of in cuts:
        steps = jax.random.uniform(jax.random.fold_in(jax.random.fold_in(own_key, 6), dim), (shards_of,), jnp.float32, least / len(cuts), high / len(cuts))
        factor_of = factor_of * jnp.repeat(jnp.exp(steps), extent[dim] // shards_of).reshape((-1,) + (1,) * (len(extent) - 1 - dim))
    return factor_of


def bell_draw(stream_key, shape, spread, most, cuts=(), kind=jnp.bfloat16):
    values = jax.random.normal(stream_key, shape, jnp.float32) * spread
    if len(cuts) > 0:
        values = block_scale(stream_key, shape, cuts, -0.22, 0.18) * values
    return jnp.clip(values, min=-most, max=most).astype(kind)


def setup_inputs(seed: int = 0) -> dict:
    streams_of = jax.random.split(jax.random.key(seed), 7)
    lattice = draw_lattice(jax.random.fold_in(streams_of[6], 71), 0)
    material = with_ends(jax.random.randint(streams_of[1], (ATOMS_ALL,), 0, TYPES), jax.random.fold_in(streams_of[1], 1), 0, TYPES - 1).astype(jnp.int32)
    polarizability = jnp.clip(jax.random.uniform(streams_of[2], (4, TYPES, WAVES), jnp.float32, -1.2, 1.2), -1.2, 1.2)
    wavenumber = jnp.clip(jnp.exp(jax.random.uniform(streams_of[3], (WAVES,), jnp.float32, math.log(2.0), math.log(3.5))), 2.0, 3.5)
    dipoles = bell_draw(streams_of[4], (WAVES, 2, 6, EXCITE, ATOMS_ALL), 1.0, 6.0, ((4, 512),))
    adjoint_in = bell_draw(streams_of[5], (WAVES, 2, 6, EXCITE, ATOMS_ALL), 1.0, 6.0, ((4, 512),))
    return dict(lattice=lattice, material=material, polarizability=polarizability, wavenumber=wavenumber, dipoles=dipoles, adjoint_in=adjoint_in)


COUPLINGS = ((0, 1, 0, 1.0), (0, 3, 1, 1.0), (0, 5, 5, 1.0), (1, 3, 0, 1.0), (1, 2, 1, 1.0), (1, 4, 5, -1.0), (2, 0, 2, 1.0), (2, 4, 4, 1.0), (2, 5, 3, -1.0), (3, 1, 3, 1.0), (3, 3, 4, 1.0), (3, 5, 2, -1.0), (4, 3, 3, 1.0), (4, 2, 4, 1.0), (4, 4, 2, 1.0), (5, 0, 5, 1.0), (5, 4, 1, -1.0), (5, 5, 0, 1.0))
KERNEL_SOURCES = ((0, (2, 5)), (1, (0, 3)), (2, (1, 4)), (3, (0, 1, 3, 4)), (4, (1, 2, 4, 5)), (5, (0, 2, 3, 5)))

def atom_polarizability(material, polarizability):
    kinds = jnp.arange(polarizability.shape[1], dtype=jnp.int32)
    onehot = (kinds[:, None] == material[None, :]).astype(jnp.float32)
    table = jnp.einsum('kyw,yn->kwn', polarizability, onehot, precision=lax.Precision.HIGHEST)
    alpha_re = jnp.stack([table[0]] * 3 + [table[2]] * 3, axis=1)[:, :, None, :]
    alpha_im = jnp.stack([table[1]] * 3 + [table[3]] * 3, axis=1)[:, :, None, :]
    return (alpha_re, alpha_im)

def pack_sources(dipoles, adjoint_in, alpha):
    alpha_re, alpha_im = alpha
    vector = adjoint_in.astype(jnp.float32)
    scaled_re = alpha_re * vector[:, 0] + alpha_im * vector[:, 1]
    scaled_im = alpha_re * vector[:, 1] - alpha_im * vector[:, 0]
    scaled = jnp.stack([scaled_re, scaled_im], axis=1).astype(jnp.bfloat16)
    return jnp.stack([dipoles, scaled], axis=1)

def green_kernels(geometry, wave):
    present, radius, unit_x, unit_y = geometry
    phase = wave * radius
    inverse = 1.0 / phase
    weight = present * inverse
    green_re = jnp.cos(phase) * weight
    green_im = jnp.sin(phase) * weight
    inv_sq = inverse * inverse
    near_re = green_re * (1.0 - inv_sq) - green_im * inverse
    near_im = green_im * (1.0 - inv_sq) + green_re * inverse
    long_re = green_re * (3.0 * inv_sq - 1.0) + 3.0 * green_im * inverse
    long_im = green_im * (3.0 * inv_sq - 1.0) - 3.0 * green_re * inverse
    cross_re = green_re - green_im * inverse
    cross_im = green_im + green_re * inverse
    xx_unit = unit_x * unit_x
    yy_unit = unit_y * unit_y
    xy_unit = unit_x * unit_y
    return jnp.stack([jnp.stack([near_re, near_im]), jnp.stack([near_re + long_re * xx_unit, near_im + long_im * xx_unit]), jnp.stack([near_re + long_re * yy_unit, near_im + long_im * yy_unit]), jnp.stack([long_re * xy_unit, long_im * xy_unit]), jnp.stack([cross_re * unit_x, cross_im * unit_x]), jnp.stack([cross_re * unit_y, cross_im * unit_y])]).astype(jnp.bfloat16)

def kernel_products(values, kernel_pair, kernel_index, components):
    sources = values.shape[-1]
    excite = values.shape[-2]
    targets = kernel_pair.shape[-1]
    count = len(components)
    picked = jnp.stack([values[:, :, comp] for comp in components]).reshape(-1, sources)
    with_re = jnp.dot(picked, kernel_pair[0], preferred_element_type=jnp.float32).reshape(count, 2, 2, excite, targets)
    with_im = jnp.dot(picked, kernel_pair[1], preferred_element_type=jnp.float32).reshape(count, 2, 2, excite, targets)
    fwd_re = with_re[:, 0, 0] - with_im[:, 0, 1]
    fwd_im = with_re[:, 0, 1] + with_im[:, 0, 0]
    adj_re = with_re[:, 1, 0] + with_im[:, 1, 1]
    adj_im = with_re[:, 1, 1] - with_im[:, 1, 0]
    if kernel_index >= 4:
        adj_re = -adj_re
        adj_im = -adj_im
    return jnp.stack([fwd_re, fwd_im, adj_re, adj_im], axis=1)

def column_fields(target_sites, source_sites, values, wavenumber, period):
    delta_x = target_sites[0][None, :] - source_sites[0][:, None]
    delta_y = target_sites[1][None, :] - source_sites[1][:, None]
    delta_y = jnp.where(2 * delta_y > period, delta_y - period, jnp.where(2 * delta_y < -period, delta_y + period, delta_y))
    delta_x = delta_x.astype(jnp.float32)
    delta_y = delta_y.astype(jnp.float32)
    radius_sq = delta_x * delta_x + delta_y * delta_y
    present = radius_sq > 0.5
    radius = jnp.sqrt(jnp.where(present, radius_sq, 1.0))
    geometry = (present.astype(jnp.float32), radius, delta_x / radius, delta_y / radius)
    targets = target_sites.shape[1]
    per_wave = []
    for wave_index in range(values.shape[0]):
        kernels = green_kernels(geometry, wavenumber[wave_index])
        products = {}
        for kernel_index, components in KERNEL_SOURCES:
            products[kernel_index] = kernel_products(values[wave_index], kernels[kernel_index], kernel_index, components)
        outputs = []
        for target_comp in range(6):
            summed = None
            for out_comp, kernel_index, source_comp, sign in COUPLINGS:
                if out_comp == target_comp:
                    place = dict(KERNEL_SOURCES)[kernel_index].index(source_comp)
                    term = sign * products[kernel_index][place]
                    summed = term if summed is None else summed + term
            outputs.append(summed)
        per_wave.append(jnp.stack(outputs, axis=1))
    return jnp.stack(per_wave).reshape(-1, targets)

def finish_outputs(fields, dipoles, adjoint_in, alpha):
    alpha_re, alpha_im = alpha
    shaped = fields.reshape((dipoles.shape[0], 2) + dipoles.shape[1:])
    forward_field = shaped[:, 0]
    adjoint_field = shaped[:, 1]
    source = dipoles.astype(jnp.float32)
    out_re = source[:, 0] - (alpha_re * forward_field[:, 0] - alpha_im * forward_field[:, 1])
    out_im = source[:, 1] - (alpha_re * forward_field[:, 1] + alpha_im * forward_field[:, 0])
    forward_out = jnp.stack([out_re, out_im], axis=1)
    adjoint_out = adjoint_in.astype(jnp.float32) - adjoint_field
    return (forward_out, adjoint_out)

def reference(lattice, material, polarizability, wavenumber, dipoles, adjoint_in):
    alpha = atom_polarizability(material, polarizability)
    values = pack_sources(dipoles, adjoint_in, alpha)
    blocks = values.reshape(values.shape[:-1] + (N_TGT, N_SRC, ATOMS))
    sites = lattice.reshape(2, N_TGT, N_SRC, ATOMS)
    period = N_SRC * TILE_Y
    field_rows = 24 * WAVES * EXCITE

    def one_column(column):
        target_sites = sites[:, :, column, :].reshape(2, N_TGT * ATOMS)

        def absorb(step, total):
            offset = step // N_TGT
            band = step % N_TGT
            source_column = (column + offset + N_SRC - 1) % N_SRC
            source_sites = sites[:, band, source_column, :]
            source_values = blocks[:, :, :, :, :, band, source_column, :]
            return total + column_fields(target_sites, source_sites, source_values, wavenumber, period)
        start_total = jnp.zeros((field_rows, N_TGT * ATOMS), jnp.float32)
        return lax.fori_loop(0, 3 * N_TGT, absorb, start_total)
    per_column = lax.map(one_column, jnp.arange(N_SRC, dtype=jnp.int32))
    per_column = per_column.reshape(N_SRC, field_rows, N_TGT, ATOMS)
    fields = jnp.transpose(per_column, (1, 2, 0, 3)).reshape(field_rows, ATOMS_ALL)
    return finish_outputs(fields, dipoles, adjoint_in, alpha)
```

```python
import functools

import jax
import jax.numpy as jnp
import ml_dtypes
import numpy as np
from jax import lax
from jax.experimental import pallas as pl
from jax.experimental.pallas import tpu as pltpu
from jax.sharding import PartitionSpec as P

MESH = pl.DeviceIdType.MESH
WAVES, EXCITE, TYPES, ATOMS = 4, 4, 16, 32
NY, NZ, NCOL, NTGT = 8, 4, 16, 32
KX, KY = 128, 64


def halves(x):
    hi = x.astype(ml_dtypes.bfloat16)
    lo = (x - hi.astype(np.float64)).astype(ml_dtypes.bfloat16)
    return hi, lo


def source_y_matrix():
    out = np.zeros((3, 128, 2, 3, 2, KY))
    ky = np.arange(KY)
    for q in range(3):
        for comp in range(6):
            for y in range(16):
                angle = 2 * np.pi * ky * ((q - 1) * 16 + y) / KY
                out[q, comp * 16 + y, 0, comp % 3, comp // 3] = np.cos(angle)
                out[q, comp * 16 + y, 1, comp % 3, comp // 3] = -np.sin(angle)
    return np.stack(halves(out.reshape(384, 768)))


def source_x_matrix():
    kx = np.arange(KX)[:, None, None, None, None]
    g, xl, ys, ri = np.meshgrid(np.arange(2), np.arange(2), np.arange(NY), np.arange(2), indexing="ij")
    unit = (1j) ** (g + ri)
    per = []
    for z in range(NZ):
        value = unit * np.exp(-2j * np.pi * kx * (8 * ys + 2 * z + xl) / KX)
        value = value.reshape(KX, 64)
        hi, lo = halves(np.concatenate([value.real, value.imag], axis=0))
        per.append(np.concatenate([hi, lo, hi], axis=1))
    return np.stack(per)


def target_x_matrix():
    xs = (2 * np.arange(NTGT)[None, :] + np.arange(2)[:, None]).reshape(64, 1)
    value = np.exp(2j * np.pi * xs * np.arange(KX) / KX)
    full = np.concatenate(
        [
            np.concatenate([value.real, -value.imag], axis=1),
            np.concatenate([value.imag, value.real], axis=1),
        ],
        axis=0,
    )
    hi, lo = halves(full)
    return np.concatenate([hi, lo], axis=1)


def target_y_matrix():
    out = np.zeros((3, 2, KY, 2, 128))
    ky = np.arange(KY)
    for comp in range(6):
        for y in range(16):
            angle = 2 * np.pi * ky * y / KY
            out[comp % 3, comp // 3, :, 0, comp * 16 + y] = np.cos(angle)
            out[comp % 3, comp // 3, :, 1, comp * 16 + y] = np.sin(angle)
    return np.stack(halves(out.reshape(384, 256) / (KX * KY)))


def table_x_matrix():
    angle = 2 * np.pi * np.arange(KX)[:, None] * np.arange(64)[None, :] / KX
    weight = np.where(np.arange(64) == 0, 1.0, 2.0)
    out = []
    for m in (np.cos(angle) * weight, 2.0 * np.sin(angle)):
        out.append(np.concatenate(halves(m), axis=1))
    return np.stack(out)


def table_y_matrix():
    angle = 2 * np.pi * np.arange(KY)[None, :] * np.arange(32)[:, None] / KY
    cos = np.cos(angle) * np.where(np.arange(32) == 0, 1.0, 2.0)[:, None]
    sin = 2.0 * np.sin(angle)
    even = np.concatenate([cos, cos], axis=1)
    odd = np.concatenate([sin, sin], axis=1)
    even_signed = np.concatenate([cos, -cos], axis=1)
    odd_signed = np.concatenate([sin, -sin], axis=1)
    groups = (
        ((0, 0, even), (1, 1, even), (2, 2, even), (3, 3, even)),
        ((0, 0, even), (1, 1, even), (3, 2, odd_signed), (2, 3, -odd_signed)),
        ((0, 0, -odd), (1, 1, -odd), (3, 2, even_signed), (2, 3, -even_signed)),
    )
    out = []
    for group in groups:
        full = np.zeros((4, 32, 4, 128))
        for array, table, matrix in group:
            full[array, :, table, :] = matrix
        hi, lo = halves(full.reshape(128, 512))
        out.append(np.concatenate([hi, lo, hi], axis=0))
    return np.stack(out)


K0, KAA, KBB, KYS, KXYT, KXS = 0, 2, 4, 6, 8, 10


def split_up(x):
    hi = x.astype(jnp.bfloat16)
    lo = (x - hi.astype(jnp.float32)).astype(jnp.bfloat16)
    return hi, lo


def dot(a, b):
    return jnp.dot(a, b, preferred_element_type=jnp.float32)


def build_tables(wave, sigma, cx, cy, tables):
    lane = lax.broadcasted_iota(jnp.int32, (64, 128), 1)
    dx = lax.broadcasted_iota(jnp.int32, (64, 128), 0).astype(jnp.float32)
    dy = (lane % 32).astype(jnp.float32)
    quarter = lane // 32
    radius_sq = dx * dx + dy * dy
    present = radius_sq > 0.5
    radius = jnp.sqrt(jnp.where(present, radius_sq, 1.0))
    unit_x = dx / radius
    unit_y = dy / radius
    phase = wave * radius
    inverse = 1.0 / phase
    weight = jnp.where(present, inverse, 0.0)
    green_re = jnp.cos(phase) * weight
    green_im = jnp.sin(phase) * weight
    inv_sq = inverse * inverse
    near_re = green_re * (1.0 - inv_sq) - green_im * inverse
    near_im = green_im * (1.0 - inv_sq) + green_re * inverse
    long_re = green_re * (3.0 * inv_sq - 1.0) + 3.0 * green_im * inverse
    long_im = green_im * (3.0 * inv_sq - 1.0) - 3.0 * green_re * inverse
    cross_re = green_re - green_im * inverse
    cross_im = green_im + green_re * inverse

    def group(a, b, c, d):
        return jnp.where(
            quarter == 0, a, jnp.where(quarter == 1, b, jnp.where(quarter == 2, c, d))
        ).astype(jnp.bfloat16)

    xx, yy, xy = unit_x * unit_x, unit_y * unit_y, unit_x * unit_y
    groups = (
        (
            0,
            group(
                near_re,
                sigma * near_im,
                near_re + long_re * xx,
                sigma * (near_im + long_im * xx),
            ),
        ),
        (
            0,
            group(
                near_re + long_re * yy,
                sigma * (near_im + long_im * yy),
                sigma * (cross_re * unit_y),
                cross_im * unit_y,
            ),
        ),
        (
            1,
            group(
                long_re * xy,
                sigma * (long_im * xy),
                sigma * (cross_re * unit_x),
                cross_im * unit_x,
            ),
        ),
    )
    for n, (parity, values) in enumerate(groups):
        along_x = dot(cx[parity], jnp.concatenate([values, values], axis=0))
        hi, lo = split_up(along_x)
        full = dot(jnp.concatenate([hi, hi, lo], axis=1), cy[n])
        for k in range(4):
            tables[4 * n + k] = full[:, k * 128 : (k + 1) * 128]


def pointwise(xa, z_ref, tables, e):
    rows = 16

    def body(i, carry):
        at = pl.multiple_of(i * rows, rows)
        top, low = pl.ds(at, rows), pl.ds(at + KX, rows)
        table = [tables[k, top, :] for k in range(12)]
        parts = [
            (xa[e, top, j * 128 : (j + 1) * 128], xa[e, low, j * 128 : (j + 1) * 128])
            for j in range(3)
        ]
        swapped = [(pltpu.roll(a, 64, 1), pltpu.roll(b, 64, 1)) for a, b in parts]

        def combine(terms):
            re = im = None
            for sign, k, (vr, vi) in terms:
                kr, ki = table[k], table[k + 1]
                tr, ti = kr * vr - ki * vi, kr * vi + ki * vr
                if re is None:
                    re, im = tr, ti
                elif sign > 0:
                    re, im = re + tr, im + ti
                else:
                    re, im = re - tr, im - ti
            return re, im

        sums = (
            combine(((1, KAA, parts[0]), (1, KXYT, parts[1]), (1, KYS, swapped[2]))),
            combine(((1, KXYT, parts[0]), (1, KBB, parts[1]), (-1, KXS, swapped[2]))),
            combine(((1, K0, parts[2]), (1, KXS, swapped[1]), (-1, KYS, swapped[0]))),
        )
        for j, (re, im) in enumerate(sums):
            z_ref[e, top, j * 128 : (j + 1) * 128] = re.astype(jnp.bfloat16)
            z_ref[e, low, j * 128 : (j + 1) * 128] = im.astype(jnp.bfloat16)
        return carry

    lax.fori_loop(0, KX // rows, body, 0)


def kernel(
    lat_h, mat_h, pol_h, wn_h, dip_h, adj_h, by_h, bx_h, tx_h, ty_h, cx_h, cy_h,
    gf_ref, ga_ref,
    lat, mat, pol, wn, dip, adj, by, bx, tx, ty, cx, cy,
    vec, mixed, send1, recv1, xb, tables, xa, z_ref, out, send2, recv2, summed, place,
    in_sem, send_sem1, recv_sem1, send_sem2, recv_sem2,
):
    t = lax.axis_index("tgt")
    col = lax.axis_index("src")
    y, z = t // NZ, lax.rem(t, NZ)
    cols = [lax.rem(col + NCOL - 1, NCOL), col, lax.rem(col + 1, NCOL)]

    barrier = pltpu.get_barrier_semaphore()
    for step in range(1, NZ):
        pl.semaphore_signal(
            barrier, inc=1, device_id={"tgt": y * NZ + lax.rem(z + step, NZ)}, device_id_type=MESH
        )
    for step in range(NY):
        peer = lax.rem(y + step, NY) * NZ + z
        for q in range(3):
            if step or q != 1:
                pl.semaphore_signal(
                    barrier, inc=1, device_id={"tgt": peer, "src": cols[q]}, device_id_type=MESH
                )

    loads = [
        pltpu.make_async_copy(src, dst, in_sem.at[n])
        for n, (src, dst) in enumerate(
            (
                (lat_h, lat),
                (mat_h, mat),
                (pol_h, pol),
                (wn_h, wn),
                (dip_h, dip),
                (adj_h, adj),
                (cx_h, cx),
                (cy_h, cy),
                (by_h, by),
                (bx_h.at[z], bx),
                (tx_h, tx),
                (ty_h, ty),
            )
        )
    ]
    for load in loads:
        load.start()
    for load in loads[:6]:
        load.wait()

    kinds = lax.broadcasted_iota(jnp.int32, (TYPES, ATOMS), 0)
    onehot = (kinds == mat[...]).astype(jnp.float32)
    alpha = [
        jnp.dot(pol[k], onehot, precision=lax.Precision.HIGHEST, preferred_element_type=jnp.float32)
        for k in range(4)
    ]

    site = (lat[0:1, :] - 2 * t) * 16 + (lat[1:2, :] - 16 * col)
    row = lax.broadcasted_iota(jnp.int32, (256, ATOMS), 0)
    same = (row // 128) * 16 + row % 16 == site
    owner = (row % 128) // 16
    for comp in range(6):
        place[comp] = (same & (owner == comp)).astype(jnp.bfloat16)

    for w in range(WAVES):
        for comp in range(6):
            ar = alpha[2 * (comp // 3)][w : w + 1, :]
            ai = alpha[2 * (comp // 3) + 1][w : w + 1, :]
            vr = adj[w, 0, comp].astype(jnp.float32)
            vi = adj[w, 1, comp].astype(jnp.float32)
            vec[comp, w * 16 : w * 16 + 4, :] = dip[w, 0, comp].astype(jnp.float32)
            vec[comp, w * 16 + 4 : w * 16 + 8, :] = dip[w, 1, comp].astype(jnp.float32)
            vec[comp, w * 16 + 8 : w * 16 + 12, :] = ar * vr + ai * vi
            vec[comp, w * 16 + 12 : w * 16 + 16, :] = ar * vi - ai * vr
    placed = None
    for comp in range(6):
        term = lax.dot_general(
            vec[comp].astype(jnp.bfloat16),
            place[comp],
            (((1,), (1,)), ((), ())),
            preferred_element_type=jnp.float32,
        )
        placed = term if placed is None else placed + term
    for xl in range(2):
        mixed[pl.ds(xl, 64, stride=2), :] = placed[:, xl * 128 : (xl + 1) * 128]
    send1[...] = mixed[...].astype(jnp.bfloat16).reshape(NY, 16, 128)

    pl.semaphore_wait(barrier, NZ - 1 + 3 * NY - 1)

    for step in range(NY):
        to = lax.rem(y + NY // 2 + step, NY)
        for q in (0, 2, 1):
            if step != NY // 2 or q != 1:
                pltpu.make_async_remote_copy(
                    src_ref=send1.at[to],
                    dst_ref=recv1.at[(2 - q) * NY + y],
                    send_sem=send_sem1,
                    recv_sem=recv_sem1,
                    device_id={"tgt": to * NZ + z, "src": cols[q]},
                    device_id_type=MESH,
                ).start()
    recv1[NY + y] = send1[y]

    for load in loads[6:]:
        load.wait()
    wave = wn[y // 2]
    sigma = (1 - 2 * lax.rem(y, 2)).astype(jnp.float32)
    build_tables(wave, sigma, cx, cy, tables)

    blocks = recv1.at[pl.ds(0, 3 * NY - 1)]
    pltpu.make_async_copy(blocks, blocks, recv_sem1).wait()

    arrived = jnp.concatenate(
        [recv1[q * NY : (q + 1) * NY].reshape(128, 128) for q in range(3)], axis=1
    )
    along_y = dot(arrived, by[0]) + dot(arrived, by[1])
    for n in range(6):
        xb[n] = along_y[:, n * 128 : (n + 1) * 128]
    for e in range(EXCITE):
        parts = []
        for g in range(2):
            for xl in range(2):
                parts.append(
                    jnp.concatenate(
                        [xb[3 * g + j, pl.ds(2 * e + xl, 16, stride=8), :] for j in range(3)],
                        axis=1,
                    )
                )
        hi, lo = split_up(jnp.concatenate(parts, axis=0))
        xa[e] = dot(bx[...], jnp.concatenate([hi, hi, lo], axis=0))
    for e in range(EXCITE):
        pointwise(xa, z_ref, tables, e)
    for e in range(EXCITE):
        value = z_ref[e]
        back_x = dot(tx[...], jnp.concatenate([value, value], axis=0))
        hi, lo = split_up(back_x)
        back = dot(hi, ty[0]) + dot(hi, ty[1]) + dot(lo, ty[0])
        re = back[:64, :128] - back[64:, 128:]
        im = back[64:, :128] + back[:64, 128:]
        for xl in range(2):
            out[pl.ds(2 * e + xl, NTGT, stride=16), :] = re[xl * 32 : (xl + 1) * 32]
            out[pl.ds(8 + 2 * e + xl, NTGT, stride=16), :] = im[xl * 32 : (xl + 1) * 32]
    send2[...] = out[...].astype(jnp.bfloat16).reshape(NTGT, 16, 128)

    for step in range(1, NTGT):
        to = lax.rem(t + step, NTGT)
        pltpu.make_async_remote_copy(
            src_ref=send2.at[to],
            dst_ref=recv2.at[t],
            send_sem=send_sem2,
            recv_sem=recv_sem2,
            device_id={"tgt": to},
            device_id_type=MESH,
        ).start()
    recv2[t] = send2[t]
    blocks = recv2.at[pl.ds(0, NTGT - 1)]
    pltpu.make_async_copy(blocks, blocks, recv_sem2).wait()

    for p in range(NY):
        total = recv2[NZ * p].astype(jnp.float32)
        for k in range(1, NZ):
            total = total + recv2[NZ * p + k].astype(jnp.float32)
        summed[p * 16 : (p + 1) * 16, :] = total
    both = jnp.concatenate([summed[pl.ds(xl, 64, stride=2), :] for xl in range(2)], axis=1)
    hi, lo = split_up(both)
    for comp in range(6):
        field = dot(hi, place[comp]) + dot(lo, place[comp])
        for w in range(WAVES):
            ar = alpha[2 * (comp // 3)][w : w + 1, :]
            ai = alpha[2 * (comp // 3) + 1][w : w + 1, :]
            fr = field[w * 16 : w * 16 + 4]
            fi = field[w * 16 + 4 : w * 16 + 8]
            gf_ref[w, 0, comp] = ar * fr - ai * fi
            gf_ref[w, 1, comp] = ar * fi + ai * fr
            ga_ref[w, 0, comp] = field[w * 16 + 8 : w * 16 + 12]
            ga_ref[w, 1, comp] = field[w * 16 + 12 : w * 16 + 16]

    blocks = send1.at[pl.ds(0, NY)]
    for _ in range(2):
        pltpu.make_async_copy(blocks, blocks, send_sem1).wait()
    blocks = send1.at[pl.ds(0, NY - 1)]
    pltpu.make_async_copy(blocks, blocks, send_sem1).wait()
    blocks = send2.at[pl.ds(0, NTGT - 1)]
    pltpu.make_async_copy(blocks, blocks, send_sem2).wait()


def per_device(lattice, material, polarizability, wavenumber, dipoles, adjoint_in):
    f32, bf16 = jnp.float32, jnp.bfloat16
    constants = [
        jnp.asarray(make())
        for make in (
            source_y_matrix, source_x_matrix, target_x_matrix, target_y_matrix, table_x_matrix, table_y_matrix,
        )
    ]
    operands = [
        lattice,
        material.reshape(1, ATOMS),
        jnp.transpose(polarizability, (0, 2, 1)),
        wavenumber,
        dipoles,
        adjoint_in,
        *constants,
    ]
    field_shape = jax.ShapeDtypeStruct(dipoles.shape, f32)
    staged = [
        pltpu.SMEM(v.shape, v.dtype) if n == 3 else pltpu.VMEM(v.shape[1:] if n == 7 else v.shape, v.dtype)
        for n, v in enumerate(operands)
    ]
    from_forward, from_adjoint = pl.pallas_call(
        kernel,
        out_shape=(field_shape, field_shape),
        in_specs=[pl.BlockSpec(memory_space=pl.ANY)] * len(operands),
        out_specs=(pl.BlockSpec(memory_space=pltpu.VMEM),) * 2,
        scratch_shapes=staged
        + [
            pltpu.VMEM((6, 64, ATOMS), f32),
            pltpu.VMEM((128, 128), f32),
            pltpu.VMEM((NY, 16, 128), bf16),
            pltpu.VMEM((3 * NY, 16, 128), bf16),
            pltpu.VMEM((6, 128, 128), f32),
            pltpu.VMEM((12, KX, 128), f32),
            pltpu.VMEM((EXCITE, 2 * KX, 384), f32),
            pltpu.VMEM((EXCITE, 2 * KX, 384), bf16),
            pltpu.VMEM((512, 128), f32),
            pltpu.VMEM((NTGT, 16, 128), bf16),
            pltpu.VMEM((NTGT, 16, 128), bf16),
            pltpu.VMEM((128, 128), f32),
            pltpu.VMEM((6, 256, ATOMS), bf16),
            pltpu.SemaphoreType.DMA((12,)),
            pltpu.SemaphoreType.DMA,
            pltpu.SemaphoreType.DMA,
            pltpu.SemaphoreType.DMA,
            pltpu.SemaphoreType.DMA,
        ],
        compiler_params=pltpu.CompilerParams(
            collective_id=0, has_side_effects=True, vmem_limit_bytes=40 * 1024 * 1024
        ),
    )(*operands)
    forward_out = dipoles.astype(f32) - from_forward
    adjoint_out = adjoint_in.astype(f32) - from_adjoint
    return forward_out, adjoint_out


def solution(mesh):
    spec = P(None, None, None, None, ("tgt", "src"))
    in_specs = (P(None, ("tgt", "src")), P(("tgt", "src")), P(), P(), spec, spec)
    return jax.shard_map(
        per_device, mesh=mesh, in_specs=in_specs, out_specs=(spec, spec), check_vma=False
    )
```

```python
import functools

import jax
import jax.numpy as jnp
import ml_dtypes
import numpy as np
from jax import lax
from jax.experimental import pallas as pl
from jax.experimental.pallas import tpu as pltpu
from jax.sharding import PartitionSpec as P

MESH = pl.DeviceIdType.MESH
WAVES, EXCITE, TYPES, ATOMS = 4, 4, 16, 32
NY, NZ, NCOL, NTGT = 8, 4, 16, 32
KX, KY = 128, 64


def halves(x):
    hi = x.astype(ml_dtypes.bfloat16)
    lo = (x - hi.astype(np.float64)).astype(ml_dtypes.bfloat16)
    return hi, lo


def source_y_matrix():
    out = np.zeros((3, 128, 2, 3, 2, KY))
    ky = np.arange(KY)
    for q in range(3):
        for comp in range(6):
            for y in range(16):
                angle = 2 * np.pi * ky * ((q - 1) * 16 + y) / KY
                out[q, comp * 16 + y, 0, comp % 3, comp // 3] = np.cos(angle)
                out[q, comp * 16 + y, 1, comp % 3, comp // 3] = -np.sin(angle)
    return np.stack(halves(out.reshape(384, 768)))


def source_x_matrix():
    kx = np.arange(KX)[:, None, None, None, None]
    g, xl, ys, ri = np.meshgrid(np.arange(2), np.arange(2), np.arange(NY), np.arange(2), indexing="ij")
    unit = (1j) ** (g + ri)
    per = []
    for z in range(NZ):
        value = unit * np.exp(-2j * np.pi * kx * (8 * ys + 2 * z + xl) / KX)
        value = value.reshape(KX, 64)
        hi, lo = halves(np.concatenate([value.real, value.imag], axis=0))
        per.append(np.concatenate([hi, lo, hi], axis=1))
    return np.stack(per)


def target_x_matrix():
    xs = (2 * np.arange(NTGT)[None, :] + np.arange(2)[:, None]).reshape(64, 1)
    value = np.exp(2j * np.pi * xs * np.arange(KX) / KX)
    full = np.concatenate(
        [
            np.concatenate([value.real, -value.imag], axis=1),
            np.concatenate([value.imag, value.real], axis=1),
        ],
        axis=0,
    )
    hi, lo = halves(full)
    return np.concatenate([hi, lo], axis=1)


def target_y_matrix():
    out = np.zeros((3, 2, KY, 2, 128))
    ky = np.arange(KY)
    for comp in range(6):
        for y in range(16):
            angle = 2 * np.pi * ky * y / KY
            out[comp % 3, comp // 3, :, 0, comp * 16 + y] = np.cos(angle)
            out[comp % 3, comp // 3, :, 1, comp * 16 + y] = np.sin(angle)
    return np.stack(halves(out.reshape(384, 256) / (KX * KY)))


def table_x_matrix():
    angle = 2 * np.pi * np.arange(KX)[:, None] * np.arange(64)[None, :] / KX
    weight = np.where(np.arange(64) == 0, 1.0, 2.0)
    out = []
    for m in (np.cos(angle) * weight, 2.0 * np.sin(angle)):
        out.append(np.concatenate(halves(m), axis=1))
    return np.stack(out)


def table_y_matrix():
    angle = 2 * np.pi * np.arange(KY)[None, :] * np.arange(32)[:, None] / KY
    cos = np.cos(angle) * np.where(np.arange(32) == 0, 1.0, 2.0)[:, None]
    sin = 2.0 * np.sin(angle)
    even = np.concatenate([cos, cos], axis=1)
    odd = np.concatenate([sin, sin], axis=1)
    even_signed = np.concatenate([cos, -cos], axis=1)
    odd_signed = np.concatenate([sin, -sin], axis=1)
    groups = (
        ((0, 0, even), (1, 1, even), (2, 2, even), (3, 3, even)),
        ((0, 0, even), (1, 1, even), (3, 2, odd_signed), (2, 3, -odd_signed)),
        ((0, 0, -odd), (1, 1, -odd), (3, 2, even_signed), (2, 3, -even_signed)),
    )
    out = []
    for group in groups:
        full = np.zeros((4, 32, 4, 128))
        for array, table, matrix in group:
            full[array, :, table, :] = matrix
        hi, lo = halves(full.reshape(128, 512))
        out.append(np.concatenate([hi, lo, hi], axis=0))
    return np.stack(out)


K0, KAA, KBB, KYS, KXYT, KXS = 0, 2, 4, 6, 8, 10


def split_up(x):
    hi = x.astype(jnp.bfloat16)
    lo = (x - hi.astype(jnp.float32)).astype(jnp.bfloat16)
    return hi, lo


def dot(a, b):
    return jnp.dot(a, b, preferred_element_type=jnp.float32)


def build_tables(wave, sigma, cx, cy, tables):
    lane = lax.broadcasted_iota(jnp.int32, (64, 128), 1)
    dx = lax.broadcasted_iota(jnp.int32, (64, 128), 0).astype(jnp.float32)
    dy = (lane % 32).astype(jnp.float32)
    quarter = lane // 32
    radius_sq = dx * dx + dy * dy
    present = radius_sq > 0.5
    radius = jnp.sqrt(jnp.where(present, radius_sq, 1.0))
    unit_x = dx / radius
    unit_y = dy / radius
    phase = wave * radius
    inverse = 1.0 / phase
    weight = jnp.where(present, inverse, 0.0)
    green_re = jnp.cos(phase) * weight
    green_im = jnp.sin(phase) * weight
    inv_sq = inverse * inverse
    near_re = green_re * (1.0 - inv_sq) - green_im * inverse
    near_im = green_im * (1.0 - inv_sq) + green_re * inverse
    long_re = green_re * (3.0 * inv_sq - 1.0) + 3.0 * green_im * inverse
    long_im = green_im * (3.0 * inv_sq - 1.0) - 3.0 * green_re * inverse
    cross_re = green_re - green_im * inverse
    cross_im = green_im + green_re * inverse

    def group(a, b, c, d):
        return jnp.where(
            quarter == 0, a, jnp.where(quarter == 1, b, jnp.where(quarter == 2, c, d))
        ).astype(jnp.bfloat16)

    xx, yy, xy = unit_x * unit_x, unit_y * unit_y, unit_x * unit_y
    groups = (
        (
            0,
            group(
                near_re,
                sigma * near_im,
                near_re + long_re * xx,
                sigma * (near_im + long_im * xx),
            ),
        ),
        (
            0,
            group(
                near_re + long_re * yy,
                sigma * (near_im + long_im * yy),
                sigma * (cross_re * unit_y),
                cross_im * unit_y,
            ),
        ),
        (
            1,
            group(
                long_re * xy,
                sigma * (long_im * xy),
                sigma * (cross_re * unit_x),
                cross_im * unit_x,
            ),
        ),
    )
    for n, (parity, values) in enumerate(groups):
        along_x = dot(cx[parity], jnp.concatenate([values, values], axis=0))
        hi, lo = split_up(along_x)
        full = dot(jnp.concatenate([hi, hi, lo], axis=1), cy[n])
        for k in range(4):
            tables[4 * n + k] = full[:, k * 128 : (k + 1) * 128]


def pointwise(xa, z_ref, tables, e):
    rows = 16

    def body(i, carry):
        at = pl.multiple_of(i * rows, rows)
        top, low = pl.ds(at, rows), pl.ds(at + KX, rows)
        table = [tables[k, top, :] for k in range(12)]
        parts = [
            (xa[e, top, j * 128 : (j + 1) * 128], xa[e, low, j * 128 : (j + 1) * 128])
            for j in range(3)
        ]
        swapped = [(pltpu.roll(a, 64, 1), pltpu.roll(b, 64, 1)) for a, b in parts]

        def combine(terms):
            re = im = None
            for sign, k, (vr, vi) in terms:
                kr, ki = table[k], table[k + 1]
                tr, ti = kr * vr - ki * vi, kr * vi + ki * vr
                if re is None:
                    re, im = tr, ti
                elif sign > 0:
                    re, im = re + tr, im + ti
                else:
                    re, im = re - tr, im - ti
            return re, im

        sums = (
            combine(((1, KAA, parts[0]), (1, KXYT, parts[1]), (1, KYS, swapped[2]))),
            combine(((1, KXYT, parts[0]), (1, KBB, parts[1]), (-1, KXS, swapped[2]))),
            combine(((1, K0, parts[2]), (1, KXS, swapped[1]), (-1, KYS, swapped[0]))),
        )
        for j, (re, im) in enumerate(sums):
            z_ref[e, top, j * 128 : (j + 1) * 128] = re.astype(jnp.bfloat16)
            z_ref[e, low, j * 128 : (j + 1) * 128] = im.astype(jnp.bfloat16)
        return carry

    lax.fori_loop(0, KX // rows, body, 0)


def kernel(
    lat_h, mat_h, pol_h, wn_h, dip_h, adj_h, by_h, bx_h, tx_h, ty_h, cx_h, cy_h,
    gf_ref, ga_ref,
    lat, mat, pol, wn, dip, adj, by, bx, tx, ty, cx, cy,
    vec, mixed, send1, recv1, xb, tables, xa, z_ref, out, send2, recv2, summed, place,
    in_sem, send_sem1, recv_sem1, send_sem2, recv_sem2,
):
    t = lax.axis_index("tgt")
    col = lax.axis_index("src")
    y, z = t // NZ, lax.rem(t, NZ)
    cols = [lax.rem(col + NCOL - 1, NCOL), col, lax.rem(col + 1, NCOL)]

    barrier = pltpu.get_barrier_semaphore()
    for step in range(1, NZ):
        pl.semaphore_signal(
            barrier, inc=1, device_id={"tgt": y * NZ + lax.rem(z + step, NZ)}, device_id_type=MESH
        )
    for step in range(NY):
        peer = lax.rem(y + step, NY) * NZ + z
        for q in range(3):
            if step or q != 1:
                pl.semaphore_signal(
                    barrier, inc=1, device_id={"tgt": peer, "src": cols[q]}, device_id_type=MESH
                )

    loads = [
        pltpu.make_async_copy(src, dst, in_sem.at[n])
        for n, (src, dst) in enumerate(
            (
                (lat_h, lat),
                (mat_h, mat),
                (pol_h, pol),
                (wn_h, wn),
                (dip_h, dip),
                (adj_h, adj),
                (cx_h, cx),
                (cy_h, cy),
                (by_h, by),
                (bx_h.at[z], bx),
                (tx_h, tx),
                (ty_h, ty),
            )
        )
    ]
    for load in loads:
        load.start()
    for load in loads[:6]:
        load.wait()

    kinds = lax.broadcasted_iota(jnp.int32, (TYPES, ATOMS), 0)
    onehot = (kinds == mat[...]).astype(jnp.float32)
    alpha = [
        jnp.dot(pol[k], onehot, precision=lax.Precision.HIGHEST, preferred_element_type=jnp.float32)
        for k in range(4)
    ]

    site = (lat[0:1, :] - 2 * t) * 16 + (lat[1:2, :] - 16 * col)
    row = lax.broadcasted_iota(jnp.int32, (256, ATOMS), 0)
    same = (row // 128) * 16 + row % 16 == site
    owner = (row % 128) // 16
    for comp in range(6):
        place[comp] = (same & (owner == comp)).astype(jnp.bfloat16)

    for w in range(WAVES):
        for comp in range(6):
            ar = alpha[2 * (comp // 3)][w : w + 1, :]
            ai = alpha[2 * (comp // 3) + 1][w : w + 1, :]
            vr = adj[w, 0, comp].astype(jnp.float32)
            vi = adj[w, 1, comp].astype(jnp.float32)
            vec[comp, w * 16 : w * 16 + 4, :] = dip[w, 0, comp].astype(jnp.float32)
            vec[comp, w * 16 + 4 : w * 16 + 8, :] = dip[w, 1, comp].astype(jnp.float32)
            vec[comp, w * 16 + 8 : w * 16 + 12, :] = ar * vr + ai * vi
            vec[comp, w * 16 + 12 : w * 16 + 16, :] = ar * vi - ai * vr
    placed = None
    for comp in range(6):
        term = lax.dot_general(
            vec[comp].astype(jnp.bfloat16),
            place[comp],
            (((1,), (1,)), ((), ())),
            preferred_element_type=jnp.float32,
        )
        placed = term if placed is None else placed + term
    for xl in range(2):
        mixed[pl.ds(xl, 64, stride=2), :] = placed[:, xl * 128 : (xl + 1) * 128]
    send1[...] = mixed[...].astype(jnp.bfloat16).reshape(NY, 16, 128)

    pl.semaphore_wait(barrier, NZ - 1 + 3 * NY - 1)

    for step in range(NY):
        to = lax.rem(y + NY // 2 + step, NY)
        for q in (0, 2, 1):
            if step != NY // 2 or q != 1:
                pltpu.make_async_remote_copy(
                    src_ref=send1.at[to],
                    dst_ref=recv1.at[(2 - q) * NY + y],
                    send_sem=send_sem1,
                    recv_sem=recv_sem1,
                    device_id={"tgt": to * NZ + z, "src": cols[q]},
                    device_id_type=MESH,
                ).start()
    recv1[NY + y] = send1[y]

    for load in loads[6:]:
        load.wait()
    wave = wn[y // 2]
    sigma = (1 - 2 * lax.rem(y, 2)).astype(jnp.float32)
    build_tables(wave, sigma, cx, cy, tables)

    blocks = recv1.at[pl.ds(0, 3 * NY - 1)]
    pltpu.make_async_copy(blocks, blocks, recv_sem1).wait()

    arrived = jnp.concatenate(
        [recv1[q * NY : (q + 1) * NY].reshape(128, 128) for q in range(3)], axis=1
    )
    along_y = dot(arrived, by[0]) + dot(arrived, by[1])
    for n in range(6):
        xb[n] = along_y[:, n * 128 : (n + 1) * 128]
    for e in range(EXCITE):
        parts = []
        for g in range(2):
            for xl in range(2):
                parts.append(
                    jnp.concatenate(
                        [xb[3 * g + j, pl.ds(2 * e + xl, 16, stride=8), :] for j in range(3)],
                        axis=1,
                    )
                )
        hi, lo = split_up(jnp.concatenate(parts, axis=0))
        xa[e] = dot(bx[...], jnp.concatenate([hi, hi, lo], axis=0))
    for e in range(EXCITE):
        pointwise(xa, z_ref, tables, e)
    for e in range(EXCITE):
        value = z_ref[e]
        back_x = dot(tx[...], jnp.concatenate([value, value], axis=0))
        hi, lo = split_up(back_x)
        back = dot(hi, ty[0]) + dot(hi, ty[1]) + dot(lo, ty[0])
        re = back[:64, :128] - back[64:, 128:]
        im = back[64:, :128] + back[:64, 128:]
        for xl in range(2):
            out[pl.ds(2 * e + xl, NTGT, stride=16), :] = re[xl * 32 : (xl + 1) * 32]
            out[pl.ds(8 + 2 * e + xl, NTGT, stride=16), :] = im[xl * 32 : (xl + 1) * 32]
    send2[...] = out[...].astype(jnp.bfloat16).reshape(NTGT, 16, 128)

    for step in range(1, NTGT):
        to = lax.rem(t + step, NTGT)
        pltpu.make_async_remote_copy(
            src_ref=send2.at[to],
            dst_ref=recv2.at[t],
            send_sem=send_sem2,
            recv_sem=recv_sem2,
            device_id={"tgt": to},
            device_id_type=MESH,
        ).start()
    recv2[t] = send2[t]
    blocks = recv2.at[pl.ds(0, NTGT - 1)]
    pltpu.make_async_copy(blocks, blocks, recv_sem2).wait()

    for p in range(NY):
        total = recv2[NZ * p].astype(jnp.float32)
        for k in range(1, NZ):
            total = total + recv2[NZ * p + k].astype(jnp.float32)
        summed[p * 16 : (p + 1) * 16, :] = total
    both = jnp.concatenate([summed[pl.ds(xl, 64, stride=2), :] for xl in range(2)], axis=1)
    hi, lo = split_up(both)
    for comp in range(6):
        field = dot(hi, place[comp]) + dot(lo, place[comp])
        for w in range(WAVES):
            ar = alpha[2 * (comp // 3)][w : w + 1, :]
            ai = alpha[2 * (comp // 3) + 1][w : w + 1, :]
            fr = field[w * 16 : w * 16 + 4]
            fi = field[w * 16 + 4 : w * 16 + 8]
            gf_ref[w, 0, comp] = ar * fr - ai * fi
            gf_ref[w, 1, comp] = ar * fi + ai * fr
            ga_ref[w, 0, comp] = field[w * 16 + 8 : w * 16 + 12]
            ga_ref[w, 1, comp] = field[w * 16 + 12 : w * 16 + 16]

    blocks = send1.at[pl.ds(0, NY)]
    for _ in range(2):
        pltpu.make_async_copy(blocks, blocks, send_sem1).wait()
    blocks = send1.at[pl.ds(0, NY - 1)]
    pltpu.make_async_copy(blocks, blocks, send_sem1).wait()
    blocks = send2.at[pl.ds(0, NTGT - 1)]
    pltpu.make_async_copy(blocks, blocks, send_sem2).wait()


def per_device(lattice, material, polarizability, wavenumber, dipoles, adjoint_in):
    f32, bf16 = jnp.float32, jnp.bfloat16
    constants = [
        jnp.asarray(make())
        for make in (
            source_y_matrix, source_x_matrix, target_x_matrix, target_y_matrix, table_x_matrix, table_y_matrix,
        )
    ]
    operands = [
        lattice,
        material.reshape(1, ATOMS),
        jnp.transpose(polarizability, (0, 2, 1)),
        wavenumber,
        dipoles,
        adjoint_in,
        *constants,
    ]
    field_shape = jax.ShapeDtypeStruct(dipoles.shape, f32)
    staged = [
        pltpu.SMEM(v.shape, v.dtype) if n == 3 else pltpu.VMEM(v.shape[1:] if n == 7 else v.shape, v.dtype)
        for n, v in enumerate(operands)
    ]
    from_forward, from_adjoint = pl.pallas_call(
        kernel,
        out_shape=(field_shape, field_shape),
        in_specs=[pl.BlockSpec(memory_space=pl.ANY)] * len(operands),
        out_specs=(pl.BlockSpec(memory_space=pltpu.VMEM),) * 2,
        scratch_shapes=staged
        + [
            pltpu.VMEM((6, 64, ATOMS), f32),
            pltpu.VMEM((128, 128), f32),
            pltpu.VMEM((NY, 16, 128), bf16),
            pltpu.VMEM((3 * NY, 16, 128), bf16),
            pltpu.VMEM((6, 128, 128), f32),
            pltpu.VMEM((12, KX, 128), f32),
            pltpu.VMEM((EXCITE, 2 * KX, 384), f32),
            pltpu.VMEM((EXCITE, 2 * KX, 384), bf16),
            pltpu.VMEM((512, 128), f32),
            pltpu.VMEM((NTGT, 16, 128), bf16),
            pltpu.VMEM((NTGT, 16, 128), bf16),
            pltpu.VMEM((128, 128), f32),
            pltpu.VMEM((6, 256, ATOMS), bf16),
            pltpu.SemaphoreType.DMA((12,)),
            pltpu.SemaphoreType.DMA,
            pltpu.SemaphoreType.DMA,
            pltpu.SemaphoreType.DMA,
            pltpu.SemaphoreType.DMA,
        ],
        compiler_params=pltpu.CompilerParams(
            collective_id=0, has_side_effects=True, vmem_limit_bytes=63 * 1024 * 1024
        ),
    )(*operands)
    forward_out = dipoles.astype(f32) - from_forward
    adjoint_out = adjoint_in.astype(f32) - from_adjoint
    return forward_out, adjoint_out


def solution(mesh):
    spec = P(None, None, None, None, ("tgt", "src"))
    in_specs = (P(None, ("tgt", "src")), P(("tgt", "src")), P(), P(), spec, spec)
    return jax.shard_map(
        per_device, mesh=mesh, in_specs=in_specs, out_specs=(spec, spec), check_vma=False
    )
```

```python
import functools

import jax
import jax.numpy as jnp
import ml_dtypes
import numpy as np
from jax import lax
from jax.experimental import pallas as pl
from jax.experimental.pallas import tpu as pltpu
from jax.sharding import PartitionSpec as P

MESH = pl.DeviceIdType.MESH
WAVES, EXCITE, TYPES, ATOMS = 4, 4, 16, 32
NY, NZ, NCOL, NTGT = 8, 4, 16, 32
KX, KY = 128, 64
RING = (4, 3, 5, 2, 6, 1, 7, 0)
FAR_FIRST = sorted(
    ((dy, dz) for dy in range(NY) for dz in range(NZ) if dy or dz),
    key=lambda o: -(min(o[0], NY - o[0]) + 2 * min(o[1], NZ - o[1])),
)


def halves(x):
    hi = x.astype(ml_dtypes.bfloat16)
    lo = (x - hi.astype(np.float64)).astype(ml_dtypes.bfloat16)
    return hi, lo


def source_y_matrix():
    out = np.zeros((3, 128, 2, 3, 2, KY))
    ky = np.arange(KY)
    for q in range(3):
        for comp in range(6):
            for y in range(16):
                angle = 2 * np.pi * ky * ((q - 1) * 16 + y) / KY
                out[q, comp * 16 + y, 0, comp % 3, comp // 3] = np.cos(angle)
                out[q, comp * 16 + y, 1, comp % 3, comp // 3] = -np.sin(angle)
    return np.stack(halves(out.reshape(384, 768)))


def source_x_matrix():
    kx = np.arange(KX)[:, None, None, None, None]
    g, xl, ys, ri = np.meshgrid(np.arange(2), np.arange(2), np.arange(NY), np.arange(2), indexing="ij")
    unit = (1j) ** (g + ri)
    per = []
    for z in range(NZ):
        value = unit * np.exp(-2j * np.pi * kx * (8 * ys + 2 * z + xl) / KX)
        value = value.reshape(KX, 64)
        hi, lo = halves(np.concatenate([value.real, value.imag], axis=0))
        per.append(np.concatenate([hi, lo, hi], axis=1))
    return np.stack(per)


def target_x_matrix():
    xs = (2 * np.arange(NTGT)[None, :] + np.arange(2)[:, None]).reshape(64, 1)
    value = np.exp(2j * np.pi * xs * np.arange(KX) / KX)
    full = np.concatenate(
        [
            np.concatenate([value.real, -value.imag], axis=1),
            np.concatenate([value.imag, value.real], axis=1),
        ],
        axis=0,
    )
    hi, lo = halves(full)
    return np.concatenate([hi, lo], axis=1)


def target_y_matrix():
    out = np.zeros((3, 2, KY, 2, 128))
    ky = np.arange(KY)
    for comp in range(6):
        for y in range(16):
            angle = 2 * np.pi * ky * y / KY
            out[comp % 3, comp // 3, :, 0, comp * 16 + y] = np.cos(angle)
            out[comp % 3, comp // 3, :, 1, comp * 16 + y] = np.sin(angle)
    return np.stack(halves(out.reshape(384, 256) / (KX * KY)))


def table_x_matrix():
    angle = 2 * np.pi * np.arange(KX)[:, None] * np.arange(64)[None, :] / KX
    weight = np.where(np.arange(64) == 0, 1.0, 2.0)
    out = []
    for m in (np.cos(angle) * weight, 2.0 * np.sin(angle)):
        out.append(np.concatenate(halves(m), axis=1))
    return np.stack(out)


def table_y_matrix():
    angle = 2 * np.pi * np.arange(KY)[None, :] * np.arange(32)[:, None] / KY
    cos = np.cos(angle) * np.where(np.arange(32) == 0, 1.0, 2.0)[:, None]
    sin = 2.0 * np.sin(angle)
    even = np.concatenate([cos, cos], axis=1)
    odd = np.concatenate([sin, sin], axis=1)
    even_signed = np.concatenate([cos, -cos], axis=1)
    odd_signed = np.concatenate([sin, -sin], axis=1)
    groups = (
        ((0, 0, even), (1, 1, even), (2, 2, even), (3, 3, even)),
        ((0, 0, even), (1, 1, even), (3, 2, odd_signed), (2, 3, -odd_signed)),
        ((0, 0, -odd), (1, 1, -odd), (3, 2, even_signed), (2, 3, -even_signed)),
    )
    out = []
    for group in groups:
        full = np.zeros((4, 32, 4, 128))
        for array, table, matrix in group:
            full[array, :, table, :] = matrix
        hi, lo = halves(full.reshape(128, 512))
        out.append(np.concatenate([hi, lo, hi], axis=0))
    return np.stack(out)


K0, KAA, KBB, KYS, KXYT, KXS = 0, 2, 4, 6, 8, 10


def split_up(x):
    hi = x.astype(jnp.bfloat16)
    lo = (x - hi.astype(jnp.float32)).astype(jnp.bfloat16)
    return hi, lo


def dot(a, b):
    return jnp.dot(a, b, preferred_element_type=jnp.float32)


def build_tables(wave, sigma, cx, cy, tables):
    lane = lax.broadcasted_iota(jnp.int32, (64, 128), 1)
    dx = lax.broadcasted_iota(jnp.int32, (64, 128), 0).astype(jnp.float32)
    dy = (lane % 32).astype(jnp.float32)
    quarter = lane // 32
    radius_sq = dx * dx + dy * dy
    present = radius_sq > 0.5
    radius = jnp.sqrt(jnp.where(present, radius_sq, 1.0))
    unit_x = dx / radius
    unit_y = dy / radius
    phase = wave * radius
    inverse = 1.0 / phase
    weight = jnp.where(present, inverse, 0.0)
    green_re = jnp.cos(phase) * weight
    green_im = jnp.sin(phase) * weight
    inv_sq = inverse * inverse
    near_re = green_re * (1.0 - inv_sq) - green_im * inverse
    near_im = green_im * (1.0 - inv_sq) + green_re * inverse
    long_re = green_re * (3.0 * inv_sq - 1.0) + 3.0 * green_im * inverse
    long_im = green_im * (3.0 * inv_sq - 1.0) - 3.0 * green_re * inverse
    cross_re = green_re - green_im * inverse
    cross_im = green_im + green_re * inverse

    def group(a, b, c, d):
        return jnp.where(
            quarter == 0, a, jnp.where(quarter == 1, b, jnp.where(quarter == 2, c, d))
        ).astype(jnp.bfloat16)

    xx, yy, xy = unit_x * unit_x, unit_y * unit_y, unit_x * unit_y
    groups = (
        (
            0,
            group(
                near_re,
                sigma * near_im,
                near_re + long_re * xx,
                sigma * (near_im + long_im * xx),
            ),
        ),
        (
            0,
            group(
                near_re + long_re * yy,
                sigma * (near_im + long_im * yy),
                sigma * (cross_re * unit_y),
                cross_im * unit_y,
            ),
        ),
        (
            1,
            group(
                long_re * xy,
                sigma * (long_im * xy),
                sigma * (cross_re * unit_x),
                cross_im * unit_x,
            ),
        ),
    )
    for n, (parity, values) in enumerate(groups):
        along_x = dot(cx[parity], jnp.concatenate([values, values], axis=0))
        hi, lo = split_up(along_x)
        full = dot(jnp.concatenate([hi, hi, lo], axis=1), cy[n])
        for k in range(4):
            tables[4 * n + k] = full[:, k * 128 : (k + 1) * 128]


def pointwise(xa, z_ref, tables):
    rows = 16

    def body(i, carry):
        at = pl.multiple_of(i * rows, rows)
        top, low = pl.ds(at, rows), pl.ds(at + KX, rows)
        table = [tables[k, top, :] for k in range(12)]
        for e in range(EXCITE):
            parts = [
                (xa[e, top, j * 128 : (j + 1) * 128], xa[e, low, j * 128 : (j + 1) * 128])
                for j in range(3)
            ]
            swapped = [(pltpu.roll(a, 64, 1), pltpu.roll(b, 64, 1)) for a, b in parts]

            def combine(terms):
                re = im = None
                for sign, k, (vr, vi) in terms:
                    kr, ki = table[k], table[k + 1]
                    tr, ti = kr * vr - ki * vi, kr * vi + ki * vr
                    if re is None:
                        re, im = tr, ti
                    elif sign > 0:
                        re, im = re + tr, im + ti
                    else:
                        re, im = re - tr, im - ti
                return re, im

            sums = (
                combine(((1, KAA, parts[0]), (1, KXYT, parts[1]), (1, KYS, swapped[2]))),
                combine(((1, KXYT, parts[0]), (1, KBB, parts[1]), (-1, KXS, swapped[2]))),
                combine(((1, K0, parts[2]), (1, KXS, swapped[1]), (-1, KYS, swapped[0]))),
            )
            for j, (re, im) in enumerate(sums):
                z_ref[e, top, j * 128 : (j + 1) * 128] = re.astype(jnp.bfloat16)
                z_ref[e, low, j * 128 : (j + 1) * 128] = im.astype(jnp.bfloat16)
        return carry

    lax.fori_loop(0, KX // rows, body, 0, unroll=8)


def kernel(
    lat_h, mat_h, pol_h, wn_h, dip_h, adj_h, by_h, bx_h, tx_h, ty_h, cx_h, cy_h,
    gf_ref, ga_ref,
    lat, mat, pol, wn, dip, adj, by, bx, tx, ty, cx, cy,
    vec, mixed, send1, recv1, xb, tables, xa, z_ref, out, send2, recv2, summed, place,
    in_sem, send_sem1, recv_sem1, send_sem2, recv_sem2,
):
    t = lax.axis_index("tgt")
    col = lax.axis_index("src")
    y, z = t // NZ, lax.rem(t, NZ)
    cols = [lax.rem(col + NCOL - 1, NCOL), col, lax.rem(col + 1, NCOL)]

    barrier = pltpu.get_barrier_semaphore()
    for step in RING:
        peer = lax.rem(y + step, NY) * NZ + z
        for q in (0, 2, 1):
            if step or q != 1:
                pl.semaphore_signal(
                    barrier, inc=1, device_id={"tgt": peer, "src": cols[q]}, device_id_type=MESH
                )
    for step in (2, 1, 3):
        pl.semaphore_signal(
            barrier, inc=1, device_id={"tgt": y * NZ + lax.rem(z + step, NZ)}, device_id_type=MESH
        )

    loads = [
        pltpu.make_async_copy(src, dst, in_sem.at[n])
        for n, (src, dst) in enumerate(
            (
                (lat_h, lat),
                (mat_h, mat),
                (pol_h, pol),
                (wn_h, wn),
                (dip_h, dip),
                (adj_h, adj),
                (cx_h, cx),
                (cy_h, cy),
                (by_h, by),
                (bx_h.at[z], bx),
                (tx_h, tx),
                (ty_h, ty),
            )
        )
    ]
    for load in loads:
        load.start()
    for load in loads[:6]:
        load.wait()

    kinds = lax.broadcasted_iota(jnp.int32, (TYPES, ATOMS), 0)
    onehot = (kinds == mat[...]).astype(jnp.float32)
    alpha = [
        jnp.dot(pol[k], onehot, precision=lax.Precision.HIGHEST, preferred_element_type=jnp.float32)
        for k in range(4)
    ]

    site = (lat[0:1, :] - 2 * t) * 16 + (lat[1:2, :] - 16 * col)
    row = lax.broadcasted_iota(jnp.int32, (256, ATOMS), 0)
    same = (row // 128) * 16 + row % 16 == site
    owner = (row % 128) // 16
    for comp in range(6):
        place[comp] = (same & (owner == comp)).astype(jnp.bfloat16)

    for w in range(WAVES):
        for comp in range(6):
            ar = alpha[2 * (comp // 3)][w : w + 1, :]
            ai = alpha[2 * (comp // 3) + 1][w : w + 1, :]
            vr = adj[w, 0, comp].astype(jnp.float32)
            vi = adj[w, 1, comp].astype(jnp.float32)
            vec[comp, w * 16 : w * 16 + 4, :] = dip[w, 0, comp].astype(jnp.float32)
            vec[comp, w * 16 + 4 : w * 16 + 8, :] = dip[w, 1, comp].astype(jnp.float32)
            vec[comp, w * 16 + 8 : w * 16 + 12, :] = ar * vr + ai * vi
            vec[comp, w * 16 + 12 : w * 16 + 16, :] = ar * vi - ai * vr
    placed = None
    for comp in range(6):
        term = lax.dot_general(
            vec[comp].astype(jnp.bfloat16),
            place[comp],
            (((1,), (1,)), ((), ())),
            preferred_element_type=jnp.float32,
        )
        placed = term if placed is None else placed + term
    for xl in range(2):
        mixed[pl.ds(xl, 64, stride=2), :] = placed[:, xl * 128 : (xl + 1) * 128]
    send1[...] = mixed[...].astype(jnp.bfloat16).reshape(NY, 16, 128)

    pl.semaphore_wait(barrier, NZ - 1 + 3 * NY - 1)

    for step in RING:
        to = lax.rem(y + step, NY)
        for q in (0, 2, 1):
            if step or q != 1:
                pltpu.make_async_remote_copy(
                    src_ref=send1.at[to],
                    dst_ref=recv1.at[(2 - q) * NY + y],
                    send_sem=send_sem1,
                    recv_sem=recv_sem1,
                    device_id={"tgt": to * NZ + z, "src": cols[q]},
                    device_id_type=MESH,
                ).start()
    recv1[NY + y] = send1[y]

    for load in loads[6:]:
        load.wait()
    wave = wn[y // 2]
    sigma = (1 - 2 * lax.rem(y, 2)).astype(jnp.float32)
    build_tables(wave, sigma, cx, cy, tables)

    blocks = recv1.at[pl.ds(0, 3 * NY - 1)]
    pltpu.make_async_copy(blocks, blocks, recv_sem1).wait()

    arrived = jnp.concatenate(
        [recv1[q * NY : (q + 1) * NY].reshape(128, 128) for q in range(3)], axis=1
    )
    along_y = dot(arrived, by[0]) + dot(arrived, by[1])
    for n in range(6):
        xb[n] = along_y[:, n * 128 : (n + 1) * 128]
    for e in range(EXCITE):
        parts = []
        for g in range(2):
            for xl in range(2):
                parts.append(
                    jnp.concatenate(
                        [xb[3 * g + j, pl.ds(2 * e + xl, 16, stride=8), :] for j in range(3)],
                        axis=1,
                    )
                )
        hi, lo = split_up(jnp.concatenate(parts, axis=0))
        xa[e] = dot(bx[...], jnp.concatenate([hi, hi, lo], axis=0))
    pointwise(xa, z_ref, tables)
    for e in range(EXCITE):
        value = z_ref[e]
        back_x = dot(tx[...], jnp.concatenate([value, value], axis=0))
        hi, lo = split_up(back_x)
        back = dot(hi, ty[0]) + dot(hi, ty[1]) + dot(lo, ty[0])
        re = back[:64, :128] - back[64:, 128:]
        im = back[64:, :128] + back[:64, 128:]
        for xl in range(2):
            out[pl.ds(2 * e + xl, NTGT, stride=16), :] = re[xl * 32 : (xl + 1) * 32]
            out[pl.ds(8 + 2 * e + xl, NTGT, stride=16), :] = im[xl * 32 : (xl + 1) * 32]
    send2[...] = out[...].astype(jnp.bfloat16).reshape(NTGT, 16, 128)

    for dy, dz in FAR_FIRST:
        to = lax.rem(y + dy, NY) * NZ + lax.rem(z + dz, NZ)
        pltpu.make_async_remote_copy(
            src_ref=send2.at[to],
            dst_ref=recv2.at[t],
            send_sem=send_sem2,
            recv_sem=recv_sem2,
            device_id={"tgt": to},
            device_id_type=MESH,
        ).start()
    recv2[t] = send2[t]
    blocks = recv2.at[pl.ds(0, NTGT - 1)]
    pltpu.make_async_copy(blocks, blocks, recv_sem2).wait()

    for p in range(NY):
        total = recv2[NZ * p].astype(jnp.float32)
        for k in range(1, NZ):
            total = total + recv2[NZ * p + k].astype(jnp.float32)
        summed[p * 16 : (p + 1) * 16, :] = total
    both = jnp.concatenate([summed[pl.ds(xl, 64, stride=2), :] for xl in range(2)], axis=1)
    hi, lo = split_up(both)
    for comp in range(6):
        field = dot(hi, place[comp]) + dot(lo, place[comp])
        for w in range(WAVES):
            ar = alpha[2 * (comp // 3)][w : w + 1, :]
            ai = alpha[2 * (comp // 3) + 1][w : w + 1, :]
            fr = field[w * 16 : w * 16 + 4]
            fi = field[w * 16 + 4 : w * 16 + 8]
            gf_ref[w, 0, comp] = ar * fr - ai * fi
            gf_ref[w, 1, comp] = ar * fi + ai * fr
            ga_ref[w, 0, comp] = field[w * 16 + 8 : w * 16 + 12]
            ga_ref[w, 1, comp] = field[w * 16 + 12 : w * 16 + 16]

    blocks = send1.at[pl.ds(0, NY)]
    for _ in range(2):
        pltpu.make_async_copy(blocks, blocks, send_sem1).wait()
    blocks = send1.at[pl.ds(0, NY - 1)]
    pltpu.make_async_copy(blocks, blocks, send_sem1).wait()
    blocks = send2.at[pl.ds(0, NTGT - 1)]
    pltpu.make_async_copy(blocks, blocks, send_sem2).wait()


def per_device(lattice, material, polarizability, wavenumber, dipoles, adjoint_in):
    f32, bf16 = jnp.float32, jnp.bfloat16
    constants = [
        jnp.asarray(make())
        for make in (
            source_y_matrix, source_x_matrix, target_x_matrix, target_y_matrix, table_x_matrix, table_y_matrix,
        )
    ]
    operands = [
        lattice,
        material.reshape(1, ATOMS),
        jnp.transpose(polarizability, (0, 2, 1)),
        wavenumber,
        dipoles,
        adjoint_in,
        *constants,
    ]
    field_shape = jax.ShapeDtypeStruct(dipoles.shape, f32)
    staged = [
        pltpu.SMEM(v.shape, v.dtype) if n == 3 else pltpu.VMEM(v.shape[1:] if n == 7 else v.shape, v.dtype)
        for n, v in enumerate(operands)
    ]
    from_forward, from_adjoint = pl.pallas_call(
        kernel,
        out_shape=(field_shape, field_shape),
        in_specs=[pl.BlockSpec(memory_space=pltpu.HBM)] * len(operands),
        out_specs=(pl.BlockSpec(memory_space=pltpu.VMEM),) * 2,
        scratch_shapes=staged
        + [
            pltpu.VMEM((6, 64, ATOMS), f32),
            pltpu.VMEM((128, 128), f32),
            pltpu.VMEM((NY, 16, 128), bf16),
            pltpu.VMEM((3 * NY, 16, 128), bf16),
            pltpu.VMEM((6, 128, 128), f32),
            pltpu.VMEM((12, KX, 128), f32),
            pltpu.VMEM((EXCITE, 2 * KX, 384), f32),
            pltpu.VMEM((EXCITE, 2 * KX, 384), bf16),
            pltpu.VMEM((512, 128), f32),
            pltpu.VMEM((NTGT, 16, 128), bf16),
            pltpu.VMEM((NTGT, 16, 128), bf16),
            pltpu.VMEM((128, 128), f32),
            pltpu.VMEM((6, 256, ATOMS), bf16),
            pltpu.SemaphoreType.DMA((12,)),
            pltpu.SemaphoreType.DMA,
            pltpu.SemaphoreType.DMA,
            pltpu.SemaphoreType.DMA,
            pltpu.SemaphoreType.DMA,
        ],
        compiler_params=pltpu.CompilerParams(
            collective_id=0, has_side_effects=True, vmem_limit_bytes=40 * 1024 * 1024
        ),
    )(*[pltpu.with_memory_space_constraint(v, pltpu.HBM) for v in operands])
    forward_out = dipoles.astype(f32) - from_forward
    adjoint_out = adjoint_in.astype(f32) - from_adjoint
    return forward_out, adjoint_out


def solution(mesh):
    spec = P(None, None, None, None, ("tgt", "src"))
    in_specs = (P(None, ("tgt", "src")), P(("tgt", "src")), P(), P(), spec, spec)
    return jax.shard_map(
        per_device, mesh=mesh, in_specs=in_specs, out_specs=(spec, spec), check_vma=False
    )
```

```python
import functools

import jax
import jax.numpy as jnp
import ml_dtypes
import numpy as np
from jax import lax
from jax.experimental import pallas as pl
from jax.experimental.pallas import tpu as pltpu
from jax.sharding import PartitionSpec as P

MESH = pl.DeviceIdType.MESH
WAVES, EXCITE, TYPES, ATOMS = 4, 4, 16, 32
NY, NZ, NCOL, NTGT = 8, 4, 16, 32
KX, KY = 128, 64
RING = (4, 3, 5, 2, 6, 1, 7, 0)
FAR_FIRST = sorted(
    ((dy, dz) for dy in range(NY) for dz in range(NZ)),
    key=lambda o: -(min(o[0], NY - o[0]) + (3, 3, 1, 1)[o[1]]),
)


def halves(x):
    hi = x.astype(ml_dtypes.bfloat16)
    lo = (x - hi.astype(np.float64)).astype(ml_dtypes.bfloat16)
    return hi, lo


def source_y_matrix():
    out = np.zeros((3, 128, 2, 3, 2, KY))
    ky = np.arange(KY)
    for q in range(3):
        for comp in range(6):
            for y in range(16):
                angle = 2 * np.pi * ky * ((q - 1) * 16 + y) / KY
                out[q, comp * 16 + y, 0, comp % 3, comp // 3] = np.cos(angle)
                out[q, comp * 16 + y, 1, comp % 3, comp // 3] = -np.sin(angle)
    return np.stack(halves(out.reshape(384, 768)))


def source_x_matrix():
    kx = np.arange(KX)[:, None, None, None, None]
    g, xl, ys, ri = np.meshgrid(np.arange(2), np.arange(2), np.arange(NY), np.arange(2), indexing="ij")
    unit = (1j) ** (g + ri)
    per = []
    for z in range(NZ):
        value = unit * np.exp(-2j * np.pi * kx * (8 * ys + 2 * z + xl) / KX)
        value = value.reshape(KX, 64)
        hi, lo = halves(np.concatenate([value.real, value.imag], axis=0))
        per.append(np.concatenate([hi, lo, hi], axis=1))
    return np.stack(per)


def target_x_matrix():
    xs = (2 * np.arange(NTGT)[None, :] + np.arange(2)[:, None]).reshape(64, 1)
    value = np.exp(2j * np.pi * xs * np.arange(KX) / KX)
    full = np.concatenate(
        [
            np.concatenate([value.real, -value.imag], axis=1),
            np.concatenate([value.imag, value.real], axis=1),
        ],
        axis=0,
    )
    hi, lo = halves(full)
    return np.concatenate([hi, lo], axis=1)


def target_y_matrix():
    out = np.zeros((3, 2, KY, 2, 128))
    ky = np.arange(KY)
    for comp in range(6):
        for y in range(16):
            angle = 2 * np.pi * ky * y / KY
            out[comp % 3, comp // 3, :, 0, comp * 16 + y] = np.cos(angle)
            out[comp % 3, comp // 3, :, 1, comp * 16 + y] = np.sin(angle)
    return np.stack(halves(out.reshape(384, 256) / (KX * KY)))


def table_x_matrix():
    angle = 2 * np.pi * np.arange(KX)[:, None] * np.arange(64)[None, :] / KX
    weight = np.where(np.arange(64) == 0, 1.0, 2.0)
    out = []
    for m in (np.cos(angle) * weight, 2.0 * np.sin(angle)):
        out.append(np.concatenate(halves(m), axis=1))
    return np.stack(out)


def table_y_matrix():
    angle = 2 * np.pi * np.arange(KY)[None, :] * np.arange(32)[:, None] / KY
    cos = np.cos(angle) * np.where(np.arange(32) == 0, 1.0, 2.0)[:, None]
    sin = 2.0 * np.sin(angle)
    even = np.concatenate([cos, cos], axis=1)
    odd = np.concatenate([sin, sin], axis=1)
    even_signed = np.concatenate([cos, -cos], axis=1)
    odd_signed = np.concatenate([sin, -sin], axis=1)
    groups = (
        ((0, 0, even), (1, 1, even), (2, 2, even), (3, 3, even)),
        ((0, 0, even), (1, 1, even), (3, 2, odd_signed), (2, 3, -odd_signed)),
        ((0, 0, -odd), (1, 1, -odd), (3, 2, even_signed), (2, 3, -even_signed)),
    )
    out = []
    for group in groups:
        full = np.zeros((4, 32, 4, 128))
        for array, table, matrix in group:
            full[array, :, table, :] = matrix
        hi, lo = halves(full.reshape(128, 512))
        out.append(np.concatenate([hi, lo, hi], axis=0))
    return np.stack(out)


K0, KAA, KBB, KYS, KXYT, KXS = 0, 2, 4, 6, 8, 10


def split_up(x):
    hi = x.astype(jnp.bfloat16)
    lo = (x - hi.astype(jnp.float32)).astype(jnp.bfloat16)
    return hi, lo


def dot(a, b):
    return jnp.dot(a, b, preferred_element_type=jnp.float32)


def build_tables(wave, sigma, cx, cy, tables):
    lane = lax.broadcasted_iota(jnp.int32, (64, 128), 1)
    dx = lax.broadcasted_iota(jnp.int32, (64, 128), 0).astype(jnp.float32)
    dy = (lane % 32).astype(jnp.float32)
    quarter = lane // 32
    radius_sq = dx * dx + dy * dy
    present = radius_sq > 0.5
    radius = jnp.sqrt(jnp.where(present, radius_sq, 1.0))
    unit_x = dx / radius
    unit_y = dy / radius
    phase = wave * radius
    inverse = 1.0 / phase
    weight = jnp.where(present, inverse, 0.0)
    green_re = jnp.cos(phase) * weight
    green_im = jnp.sin(phase) * weight
    inv_sq = inverse * inverse
    near_re = green_re * (1.0 - inv_sq) - green_im * inverse
    near_im = green_im * (1.0 - inv_sq) + green_re * inverse
    long_re = green_re * (3.0 * inv_sq - 1.0) + 3.0 * green_im * inverse
    long_im = green_im * (3.0 * inv_sq - 1.0) - 3.0 * green_re * inverse
    cross_re = green_re - green_im * inverse
    cross_im = green_im + green_re * inverse

    def group(a, b, c, d):
        return jnp.where(
            quarter == 0, a, jnp.where(quarter == 1, b, jnp.where(quarter == 2, c, d))
        ).astype(jnp.bfloat16)

    xx, yy, xy = unit_x * unit_x, unit_y * unit_y, unit_x * unit_y
    groups = (
        (
            0,
            group(
                near_re,
                sigma * near_im,
                near_re + long_re * xx,
                sigma * (near_im + long_im * xx),
            ),
        ),
        (
            0,
            group(
                near_re + long_re * yy,
                sigma * (near_im + long_im * yy),
                sigma * (cross_re * unit_y),
                cross_im * unit_y,
            ),
        ),
        (
            1,
            group(
                long_re * xy,
                sigma * (long_im * xy),
                sigma * (cross_re * unit_x),
                cross_im * unit_x,
            ),
        ),
    )
    for n, (parity, values) in enumerate(groups):
        along_x = dot(cx[parity], jnp.concatenate([values, values], axis=0))
        hi, lo = split_up(along_x)
        full = dot(jnp.concatenate([hi, hi, lo], axis=1), cy[n])
        for k in range(4):
            tables[4 * n + k] = full[:, k * 128 : (k + 1) * 128]


def pointwise(xa, z_ref, tables):
    rows = 16

    def body(i, carry):
        at = pl.multiple_of(i * rows, rows)
        top, low = pl.ds(at, rows), pl.ds(at + KX, rows)
        table = [tables[k, top, :] for k in range(12)]
        for e in range(EXCITE):
            parts = [
                (xa[e, top, j * 128 : (j + 1) * 128], xa[e, low, j * 128 : (j + 1) * 128])
                for j in range(3)
            ]
            swapped = [(pltpu.roll(a, 64, 1), pltpu.roll(b, 64, 1)) for a, b in parts]

            def combine(terms):
                re = im = None
                for sign, k, (vr, vi) in terms:
                    kr, ki = table[k], table[k + 1]
                    tr, ti = kr * vr - ki * vi, kr * vi + ki * vr
                    if re is None:
                        re, im = tr, ti
                    elif sign > 0:
                        re, im = re + tr, im + ti
                    else:
                        re, im = re - tr, im - ti
                return re, im

            sums = (
                combine(((1, KAA, parts[0]), (1, KXYT, parts[1]), (1, KYS, swapped[2]))),
                combine(((1, KXYT, parts[0]), (1, KBB, parts[1]), (-1, KXS, swapped[2]))),
                combine(((1, K0, parts[2]), (1, KXS, swapped[1]), (-1, KYS, swapped[0]))),
            )
            for j, (re, im) in enumerate(sums):
                z_ref[e, top, j * 128 : (j + 1) * 128] = re.astype(jnp.bfloat16)
                z_ref[e, low, j * 128 : (j + 1) * 128] = im.astype(jnp.bfloat16)
        return carry

    lax.fori_loop(0, KX // rows, body, 0, unroll=8)


def kernel(
    lat_h, mat_h, pol_h, wn_h, dip_h, adj_h, by_h, bx_h, tx_h, ty_h, cx_h, cy_h,
    gf_ref, ga_ref,
    lat, mat, pol, wn, dip, adj, by, bx, tx, ty, cx, cy,
    vec, mixed, send1, recv1, xb, tables, xa, z_ref, out, send2, recv2, summed, place,
    in_sem, send_sem1, recv_sem1, send_sem2, recv_sem2,
):
    t = lax.axis_index("tgt")
    col = lax.axis_index("src")
    y, z = t // NZ, lax.rem(t, NZ)
    z_lo = lax.rem(col // 2, 2)

    def other(b):
        return b + 2 - 4 * lax.rem(b // 2, 2)

    def around(b):
        return [lax.rem(b + NCOL - 1, NCOL), b, lax.rem(b + 1, NCOL)]

    served = other(col)
    sources = around(served)
    helpers = [other(b) for b in around(col)]

    barrier = pltpu.get_barrier_semaphore()
    for step in RING:
        peer = lax.rem(y + step, NY) * NZ + z
        for q in (0, 2, 1):
            pl.semaphore_signal(
                barrier, inc=1, device_id={"tgt": peer, "src": sources[q]}, device_id_type=MESH
            )
    for step in (2, 1, 3):
        pl.semaphore_signal(
            barrier, inc=1, device_id={"tgt": y * NZ + lax.rem(z + step, NZ)}, device_id_type=MESH
        )

    loads = [
        pltpu.make_async_copy(src, dst, in_sem.at[n])
        for n, (src, dst) in enumerate(
            (
                (lat_h, lat),
                (mat_h, mat),
                (pol_h, pol),
                (wn_h, wn),
                (dip_h, dip),
                (adj_h, adj),
                (cx_h, cx),
                (cy_h, cy),
                (by_h, by),
                (bx_h.at[z], bx),
                (tx_h, tx),
                (ty_h, ty),
            )
        )
    ]
    for load in loads:
        load.start()
    for load in loads[:6]:
        load.wait()

    kinds = lax.broadcasted_iota(jnp.int32, (TYPES, ATOMS), 0)
    onehot = (kinds == mat[...]).astype(jnp.float32)
    alpha = [
        jnp.dot(pol[k], onehot, precision=lax.Precision.HIGHEST, preferred_element_type=jnp.float32)
        for k in range(4)
    ]

    site = (lat[0:1, :] - 2 * t) * 16 + (lat[1:2, :] - 16 * col)
    row = lax.broadcasted_iota(jnp.int32, (256, ATOMS), 0)
    same = (row // 128) * 16 + row % 16 == site
    owner = (row % 128) // 16
    for comp in range(6):
        place[comp] = (same & (owner == comp)).astype(jnp.bfloat16)

    for w in range(WAVES):
        for comp in range(6):
            ar = alpha[2 * (comp // 3)][w : w + 1, :]
            ai = alpha[2 * (comp // 3) + 1][w : w + 1, :]
            vr = adj[w, 0, comp].astype(jnp.float32)
            vi = adj[w, 1, comp].astype(jnp.float32)
            vec[comp, w * 16 : w * 16 + 4, :] = dip[w, 0, comp].astype(jnp.float32)
            vec[comp, w * 16 + 4 : w * 16 + 8, :] = dip[w, 1, comp].astype(jnp.float32)
            vec[comp, w * 16 + 8 : w * 16 + 12, :] = ar * vr + ai * vi
            vec[comp, w * 16 + 12 : w * 16 + 16, :] = ar * vi - ai * vr
    placed = None
    for comp in range(6):
        term = lax.dot_general(
            vec[comp].astype(jnp.bfloat16),
            place[comp],
            (((1,), (1,)), ((), ())),
            preferred_element_type=jnp.float32,
        )
        placed = term if placed is None else placed + term
    for xl in range(2):
        mixed[pl.ds(xl, 64, stride=2), :] = placed[:, xl * 128 : (xl + 1) * 128]
    send1[...] = mixed[...].astype(jnp.bfloat16).reshape(NY, 16, 128)

    pl.semaphore_wait(barrier, NZ - 1 + 3 * NY)

    for step in RING:
        to = lax.rem(y + step, NY)
        for q in (0, 2, 1):
            pltpu.make_async_remote_copy(
                src_ref=send1.at[to],
                dst_ref=recv1.at[(2 - q) * NY + y],
                send_sem=send_sem1,
                recv_sem=recv_sem1,
                device_id={"tgt": to * NZ + z, "src": helpers[q]},
                device_id_type=MESH,
            ).start()

    for load in loads[6:]:
        load.wait()
    wave = wn[y // 2]
    sigma = (1 - 2 * lax.rem(y, 2)).astype(jnp.float32)
    build_tables(wave, sigma, cx, cy, tables)

    pltpu.make_async_copy(recv1, recv1, recv_sem1).wait()

    arrived = jnp.concatenate(
        [recv1[q * NY : (q + 1) * NY].reshape(128, 128) for q in range(3)], axis=1
    )
    along_y = dot(arrived, by[0]) + dot(arrived, by[1])
    for n in range(6):
        xb[n] = along_y[:, n * 128 : (n + 1) * 128]
    for e in range(EXCITE):
        parts = []
        for g in range(2):
            for xl in range(2):
                parts.append(
                    jnp.concatenate(
                        [xb[3 * g + j, pl.ds(2 * e + xl, 16, stride=8), :] for j in range(3)],
                        axis=1,
                    )
                )
        hi, lo = split_up(jnp.concatenate(parts, axis=0))
        xa[e] = dot(bx[...], jnp.concatenate([hi, hi, lo], axis=0))
    pointwise(xa, z_ref, tables)
    for e in range(EXCITE):
        value = z_ref[e]
        back_x = dot(tx[...], jnp.concatenate([value, value], axis=0))
        hi, lo = split_up(back_x)
        back = dot(hi, ty[0]) + dot(hi, ty[1]) + dot(lo, ty[0])
        re = back[:64, :128] - back[64:, 128:]
        im = back[64:, :128] + back[:64, 128:]
        for xl in range(2):
            out[pl.ds(2 * e + xl, NTGT, stride=16), :] = re[xl * 32 : (xl + 1) * 32]
            out[pl.ds(8 + 2 * e + xl, NTGT, stride=16), :] = im[xl * 32 : (xl + 1) * 32]
    send2[...] = out[...].astype(jnp.bfloat16).reshape(NTGT, 16, 128)

    for dy, dz in FAR_FIRST:
        to = lax.rem(y + dy, NY) * NZ + lax.rem(z + dz + 1 + z_lo, NZ)
        pltpu.make_async_remote_copy(
            src_ref=send2.at[to],
            dst_ref=recv2.at[t],
            send_sem=send_sem2,
            recv_sem=recv_sem2,
            device_id={"tgt": to, "src": served},
            device_id_type=MESH,
        ).start()
    pltpu.make_async_copy(recv2, recv2, recv_sem2).wait()

    for p in range(NY):
        total = recv2[NZ * p].astype(jnp.float32)
        for k in range(1, NZ):
            total = total + recv2[NZ * p + k].astype(jnp.float32)
        summed[p * 16 : (p + 1) * 16, :] = total
    both = jnp.concatenate([summed[pl.ds(xl, 64, stride=2), :] for xl in range(2)], axis=1)
    hi, lo = split_up(both)
    for comp in range(6):
        field = dot(hi, place[comp]) + dot(lo, place[comp])
        for w in range(WAVES):
            ar = alpha[2 * (comp // 3)][w : w + 1, :]
            ai = alpha[2 * (comp // 3) + 1][w : w + 1, :]
            fr = field[w * 16 : w * 16 + 4]
            fi = field[w * 16 + 4 : w * 16 + 8]
            gf_ref[w, 0, comp] = ar * fr - ai * fi
            gf_ref[w, 1, comp] = ar * fi + ai * fr
            ga_ref[w, 0, comp] = field[w * 16 + 8 : w * 16 + 12]
            ga_ref[w, 1, comp] = field[w * 16 + 12 : w * 16 + 16]

    for _ in range(3):
        pltpu.make_async_copy(send1, send1, send_sem1).wait()
    pltpu.make_async_copy(send2, send2, send_sem2).wait()


def per_device(lattice, material, polarizability, wavenumber, dipoles, adjoint_in):
    f32, bf16 = jnp.float32, jnp.bfloat16
    constants = [
        jnp.asarray(make())
        for make in (
            source_y_matrix, source_x_matrix, target_x_matrix, target_y_matrix, table_x_matrix, table_y_matrix,
        )
    ]
    operands = [
        lattice,
        material.reshape(1, ATOMS),
        jnp.transpose(polarizability, (0, 2, 1)),
        wavenumber,
        dipoles,
        adjoint_in,
        *constants,
    ]
    field_shape = jax.ShapeDtypeStruct(dipoles.shape, f32)
    staged = [
        pltpu.SMEM(v.shape, v.dtype) if n == 3 else pltpu.VMEM(v.shape[1:] if n == 7 else v.shape, v.dtype)
        for n, v in enumerate(operands)
    ]
    from_forward, from_adjoint = pl.pallas_call(
        kernel,
        out_shape=(field_shape, field_shape),
        in_specs=[pl.BlockSpec(memory_space=pltpu.HBM)] * len(operands),
        out_specs=(pl.BlockSpec(memory_space=pltpu.VMEM),) * 2,
        scratch_shapes=staged
        + [
            pltpu.VMEM((6, 64, ATOMS), f32),
            pltpu.VMEM((128, 128), f32),
            pltpu.VMEM((NY, 16, 128), bf16),
            pltpu.VMEM((3 * NY, 16, 128), bf16),
            pltpu.VMEM((6, 128, 128), f32),
            pltpu.VMEM((12, KX, 128), f32),
            pltpu.VMEM((EXCITE, 2 * KX, 384), f32),
            pltpu.VMEM((EXCITE, 2 * KX, 384), bf16),
            pltpu.VMEM((512, 128), f32),
            pltpu.VMEM((NTGT, 16, 128), bf16),
            pltpu.VMEM((NTGT, 16, 128), bf16),
            pltpu.VMEM((128, 128), f32),
            pltpu.VMEM((6, 256, ATOMS), bf16),
            pltpu.SemaphoreType.DMA((12,)),
            pltpu.SemaphoreType.DMA,
            pltpu.SemaphoreType.DMA,
            pltpu.SemaphoreType.DMA,
            pltpu.SemaphoreType.DMA,
        ],
        compiler_params=pltpu.CompilerParams(
            collective_id=0, has_side_effects=True, vmem_limit_bytes=40 * 1024 * 1024
        ),
    )(*[pltpu.with_memory_space_constraint(v, pltpu.HBM) for v in operands])
    forward_out = dipoles.astype(f32) - from_forward
    adjoint_out = adjoint_in.astype(f32) - from_adjoint
    return forward_out, adjoint_out


def solution(mesh):
    spec = P(None, None, None, None, ("tgt", "src"))
    in_specs = (P(None, ("tgt", "src")), P(("tgt", "src")), P(), P(), spec, spec)
    return jax.shard_map(
        per_device, mesh=mesh, in_specs=in_specs, out_specs=(spec, spec), check_vma=False
    )
```

```python
import functools

import jax
import jax.numpy as jnp
import ml_dtypes
import numpy as np
from jax import lax
from jax.experimental import pallas as pl
from jax.experimental.pallas import tpu as pltpu
from jax.sharding import PartitionSpec as P

MESH = pl.DeviceIdType.MESH
WAVES, EXCITE, TYPES, ATOMS = 4, 4, 16, 32
NY, NZ, NCOL, NTGT = 8, 4, 16, 32
KX, KY = 128, 64
RING = (4, 3, 5, 2, 6, 1, 7, 0)
FAR_FIRST = sorted(
    ((dy, dz) for dy in range(NY) for dz in range(NZ)),
    key=lambda o: -(min(o[0], NY - o[0]) + (3, 3, 1, 1)[o[1]]),
)


def halves(x):
    hi = x.astype(ml_dtypes.bfloat16)
    lo = (x - hi.astype(np.float64)).astype(ml_dtypes.bfloat16)
    return hi, lo


def source_y_matrix():
    out = np.zeros((3, 128, 2, 3, 2, KY))
    ky = np.arange(KY)
    for q in range(3):
        for comp in range(6):
            for y in range(16):
                angle = 2 * np.pi * ky * ((q - 1) * 16 + y) / KY
                out[q, comp * 16 + y, 0, comp % 3, comp // 3] = np.cos(angle)
                out[q, comp * 16 + y, 1, comp % 3, comp // 3] = -np.sin(angle)
    return np.stack(halves(out.reshape(384, 768)))


def rows_x(x):
    angle = 2 * np.pi * np.arange(64)[:, None] * x[None, :] / KX
    sine = np.sin(angle)
    sine[0] = np.cos(np.pi * x)
    return np.concatenate([np.cos(angle), sine], axis=0)


def source_x_matrix():
    ys, xl = np.meshgrid(np.arange(NY), np.arange(2), indexing="ij")
    per = []
    for z in range(NZ):
        value = rows_x((8 * ys + 2 * z + xl).reshape(-1))
        hi, lo = halves(np.concatenate([value, value], axis=1))
        per.append(np.concatenate([hi, lo, hi], axis=1))
    return np.stack(per)


def target_x_matrix():
    xs = (2 * np.arange(NTGT)[None, :] + np.arange(2)[:, None]).reshape(64)
    weight = np.full((KX, 1), 2.0)
    weight[0] = weight[64] = 1.0
    hi, lo = halves((weight * rows_x(xs)).T)
    return np.concatenate([hi, lo], axis=1)


def target_y_matrix():
    out = np.zeros((3, 2, KY, 2, 128))
    ky = np.arange(KY)
    for comp in range(6):
        for y in range(16):
            angle = 2 * np.pi * ky * y / KY
            out[comp % 3, comp // 3, :, 0, comp * 16 + y] = np.cos(angle)
            out[comp % 3, comp // 3, :, 1, comp * 16 + y] = np.sin(angle)
    return np.stack(halves(out.reshape(384, 256) / (KX * KY)))


def table_x_matrix():
    even = rows_x(np.arange(64)) * np.where(np.arange(64) == 0, 1.0, 2.0)
    odd = 2.0 * rows_x(np.arange(64))
    even[65:] = even[1:64]
    odd[64] = 0.0
    odd[:64] = odd[64:]
    return np.stack([np.concatenate(halves(m), axis=1) for m in (even, odd)])


def table_y_matrix():
    angle = 2 * np.pi * np.arange(KY)[None, :] * np.arange(32)[:, None] / KY
    cos = np.cos(angle) * np.where(np.arange(32) == 0, 1.0, 2.0)[:, None]
    sin = 2.0 * np.sin(angle)
    even = np.concatenate([cos, cos], axis=1)
    odd = np.concatenate([sin, sin], axis=1)
    even_signed = np.concatenate([cos, -cos], axis=1)
    odd_signed = np.concatenate([sin, -sin], axis=1)
    groups = (
        ((0, 0, even), (1, 1, even), (2, 2, even), (3, 3, even)),
        ((0, 0, even), (1, 1, even), (3, 2, odd_signed), (2, 3, -odd_signed)),
        ((1, 0, odd), (0, 1, -odd), (2, 2, even_signed), (3, 3, even_signed)),
    )
    out = []
    for group in groups:
        full = np.zeros((4, 32, 4, 128))
        for array, table, matrix in group:
            full[array, :, table, :] = matrix
        hi, lo = halves(full.reshape(128, 512))
        out.append(np.concatenate([hi, lo, hi], axis=0))
    return np.stack(out)


K0, KAA, KBB, KYS, KXYT, KXS = 0, 2, 4, 6, 8, 10


def split_up(x):
    hi = x.astype(jnp.bfloat16)
    lo = (x - hi.astype(jnp.float32)).astype(jnp.bfloat16)
    return hi, lo


def dot(a, b):
    return jnp.dot(a, b, preferred_element_type=jnp.float32)


def build_tables(wave, sigma, cx, cy, tables):
    lane = lax.broadcasted_iota(jnp.int32, (64, 128), 1)
    dx = lax.broadcasted_iota(jnp.int32, (64, 128), 0).astype(jnp.float32)
    dy = (lane % 32).astype(jnp.float32)
    quarter = lane // 32
    radius_sq = dx * dx + dy * dy
    present = radius_sq > 0.5
    radius = jnp.sqrt(jnp.where(present, radius_sq, 1.0))
    unit_x = dx / radius
    unit_y = dy / radius
    phase = wave * radius
    inverse = 1.0 / phase
    weight = jnp.where(present, inverse, 0.0)
    green_re = jnp.cos(phase) * weight
    green_im = jnp.sin(phase) * weight
    inv_sq = inverse * inverse
    near_re = green_re * (1.0 - inv_sq) - green_im * inverse
    near_im = green_im * (1.0 - inv_sq) + green_re * inverse
    long_re = green_re * (3.0 * inv_sq - 1.0) + 3.0 * green_im * inverse
    long_im = green_im * (3.0 * inv_sq - 1.0) - 3.0 * green_re * inverse
    cross_re = green_re - green_im * inverse
    cross_im = green_im + green_re * inverse

    def group(a, b, c, d):
        return jnp.where(
            quarter == 0, a, jnp.where(quarter == 1, b, jnp.where(quarter == 2, c, d))
        ).astype(jnp.bfloat16)

    xx, yy, xy = unit_x * unit_x, unit_y * unit_y, unit_x * unit_y
    groups = (
        (
            0,
            group(
                near_re,
                sigma * near_im,
                near_re + long_re * xx,
                sigma * (near_im + long_im * xx),
            ),
        ),
        (
            0,
            group(
                near_re + long_re * yy,
                sigma * (near_im + long_im * yy),
                sigma * (cross_re * unit_y),
                cross_im * unit_y,
            ),
        ),
        (
            1,
            group(
                long_re * xy,
                sigma * (long_im * xy),
                sigma * (cross_re * unit_x),
                cross_im * unit_x,
            ),
        ),
    )
    for n, (parity, values) in enumerate(groups):
        along_x = dot(cx[parity], jnp.concatenate([values, values], axis=0))
        hi, lo = split_up(along_x)
        full = dot(jnp.concatenate([hi, hi, lo], axis=1), cy[n])
        for k in range(4):
            tables[4 * n + k] = full[:, k * 128 : (k + 1) * 128]


def pointwise(xa, z_ref, tables):
    rows = 16

    def body(i, carry):
        at = pl.multiple_of(i * rows, rows)
        top, low = pl.ds(at, rows), pl.ds(at + 64, rows)
        even_top = {k: (tables[k, top, :], tables[k + 1, top, :]) for k in (K0, KAA, KBB, KYS)}
        even_low = {k: (tables[k, low, :], tables[k + 1, low, :]) for k in (K0, KAA, KBB, KYS)}
        odd = {k: (tables[k, top, :], tables[k + 1, top, :]) for k in (KXYT, KXS)}
        for e in range(EXCITE):

            def part(rows_of, j):
                return tuple(
                    xa[e, rows_of, c * 384 + j * 128 : c * 384 + (j + 1) * 128] for c in range(2)
                )

            cos = [part(top, j) for j in range(3)]
            sin = [part(low, j) for j in range(3)]
            cos_swapped = [(pltpu.roll(a, 64, 1), pltpu.roll(b, 64, 1)) for a, b in cos]
            sin_swapped = [(pltpu.roll(a, 64, 1), pltpu.roll(b, 64, 1)) for a, b in sin]

            def combine(terms):
                re = im = None
                for sign, (kr, ki), (vr, vi) in terms:
                    tr, ti = kr * vr - ki * vi, kr * vi + ki * vr
                    if re is None:
                        re, im = tr, ti
                    elif sign > 0:
                        re, im = re + tr, im + ti
                    else:
                        re, im = re - tr, im - ti
                return re, im

            for rows_of, even, own, own_sw, cross, cross_sw, s in (
                (top, even_top, cos, cos_swapped, sin, sin_swapped, -1),
                (low, even_low, sin, sin_swapped, cos, cos_swapped, 1),
            ):
                sums = (
                    ((1, even[KAA], own[0]), (s, odd[KXYT], cross[1]), (1, even[KYS], own_sw[2])),
                    ((1, even[KBB], own[1]), (s, odd[KXYT], cross[0]), (-s, odd[KXS], cross_sw[2])),
                    ((1, even[K0], own[2]), (s, odd[KXS], cross_sw[1]), (-1, even[KYS], own_sw[0])),
                )
                for j, terms in enumerate(sums):
                    for c, value in enumerate(combine(terms)):
                        z_ref[e, rows_of, c * 384 + j * 128 : c * 384 + (j + 1) * 128] = (
                            value.astype(jnp.bfloat16)
                        )
        return carry

    lax.fori_loop(0, 64 // rows, body, 0, unroll=4)


def kernel(
    lat_h, mat_h, pol_h, wn_h, dip_h, adj_h, by_h, bx_h, tx_h, ty_h, cx_h, cy_h,
    gf_ref, ga_ref,
    lat, mat, pol, wn, dip, adj, by, bx, tx, ty, cx, cy,
    vec, send1, recv1, xb, tables, xa, z_ref, out, send2, recv2, place,
    in_sem, send_sem1, recv_sem1, send_sem2, recv_sem2,
):
    t = lax.axis_index("tgt")
    col = lax.axis_index("src")
    y, z = t // NZ, lax.rem(t, NZ)
    z_lo = lax.rem(col // 2, 2)

    def other(b):
        return b + 2 - 4 * lax.rem(b // 2, 2)

    def around(b):
        return [lax.rem(b + NCOL - 1, NCOL), b, lax.rem(b + 1, NCOL)]

    served = other(col)
    sources = around(served)
    helpers = [other(b) for b in around(col)]

    barrier = pltpu.get_barrier_semaphore()
    for step in RING:
        peer = lax.rem(y + step, NY) * NZ + z
        for q in (0, 2, 1):
            pl.semaphore_signal(
                barrier, inc=1, device_id={"tgt": peer, "src": sources[q]}, device_id_type=MESH
            )
    for step in (2, 1, 3):
        pl.semaphore_signal(
            barrier, inc=1, device_id={"tgt": y * NZ + lax.rem(z + step, NZ)}, device_id_type=MESH
        )

    loads = [
        pltpu.make_async_copy(src, dst, in_sem.at[n])
        for n, (src, dst) in enumerate(
            (
                (lat_h, lat),
                (mat_h, mat),
                (pol_h, pol),
                (wn_h, wn),
                (dip_h, dip),
                (adj_h, adj),
                (cx_h, cx),
                (cy_h, cy),
                (by_h, by),
                (bx_h.at[z], bx),
                (tx_h, tx),
                (ty_h, ty),
            )
        )
    ]
    for load in loads:
        load.start()
    for load in loads[:6]:
        load.wait()

    kinds = lax.broadcasted_iota(jnp.int32, (TYPES, ATOMS), 0)
    onehot = (kinds == mat[...]).astype(jnp.float32)
    alpha = [
        jnp.dot(pol[k], onehot, precision=lax.Precision.HIGHEST, preferred_element_type=jnp.float32)
        for k in range(4)
    ]

    site = (lat[0:1, :] - 2 * t) * 16 + (lat[1:2, :] - 16 * col)
    row = lax.broadcasted_iota(jnp.int32, (256, ATOMS), 0)
    same = (row // 128) * 16 + row % 16 == site
    owner = (row % 128) // 16
    for comp in range(6):
        place[comp] = (same & (owner == comp)).astype(jnp.bfloat16)

    for w in range(WAVES):
        for comp in range(6):
            ar = alpha[2 * (comp // 3)][w : w + 1, :]
            ai = alpha[2 * (comp // 3) + 1][w : w + 1, :]
            vr = adj[w, 0, comp].astype(jnp.float32)
            vi = adj[w, 1, comp].astype(jnp.float32)
            vec[comp, w * 16 : w * 16 + 4, :] = dip[w, 0, comp].astype(jnp.float32)
            vec[comp, w * 16 + 4 : w * 16 + 8, :] = dip[w, 1, comp].astype(jnp.float32)
            vec[comp, w * 16 + 8 : w * 16 + 12, :] = ar * vr + ai * vi
            vec[comp, w * 16 + 12 : w * 16 + 16, :] = ar * vi - ai * vr
    placed = None
    for comp in range(6):
        term = lax.dot_general(
            vec[comp].astype(jnp.bfloat16),
            place[comp],
            (((1,), (1,)), ((), ())),
            preferred_element_type=jnp.float32,
        )
        placed = term if placed is None else placed + term
    for p in range(NY):
        part = placed[p * 8 : (p + 1) * 8]
        send1[p] = jnp.concatenate([part[:, :128], part[:, 128:]], axis=0).astype(jnp.bfloat16)

    pl.semaphore_wait(barrier, NZ - 1 + 3 * NY)

    for step in RING:
        to = lax.rem(y + step, NY)
        for q in (0, 2, 1):
            pltpu.make_async_remote_copy(
                src_ref=send1.at[to],
                dst_ref=recv1.at[(2 - q) * NY + y],
                send_sem=send_sem1,
                recv_sem=recv_sem1,
                device_id={"tgt": to * NZ + z, "src": helpers[q]},
                device_id_type=MESH,
            ).start()

    for load in loads[6:]:
        load.wait()
    wave = wn[y // 2]
    sigma = (1 - 2 * lax.rem(y, 2)).astype(jnp.float32)
    build_tables(wave, sigma, cx, cy, tables)

    pltpu.make_async_copy(recv1, recv1, recv_sem1).wait()

    arrived = jnp.concatenate(
        [recv1[q * NY : (q + 1) * NY].reshape(128, 128) for q in range(3)], axis=1
    )
    along_y = dot(jnp.concatenate([arrived, arrived], axis=1), by[...].reshape(768, 768))
    for n in range(6):
        xb[n, :128, :] = along_y[:, n * 128 : (n + 1) * 128]
    for e in range(EXCITE):
        sums = [
            [
                jnp.concatenate(
                    [xb[3 * g + j, pl.ds(4 * ri + e, 16, stride=8), :] for j in range(3)], axis=1
                )
                for ri in range(2)
            ]
            for g in range(2)
        ]
        real = jnp.concatenate([sums[0][0], -sums[1][1]], axis=0)
        imag = jnp.concatenate([sums[0][1], sums[1][0]], axis=0)
        hi, lo = split_up(jnp.concatenate([real, imag], axis=1))
        xa[e] = dot(bx[...], jnp.concatenate([hi, hi, lo], axis=0))
    pointwise(xa, z_ref, tables)
    back_x = []
    for e in range(EXCITE):
        value = z_ref[e]
        along = dot(tx[...], jnp.concatenate([value, value], axis=0)).astype(jnp.bfloat16)
        back_x.append(jnp.concatenate([along[:, :384], along[:, 384:]], axis=0))
    back_x = jnp.concatenate(back_x, axis=0)
    back = dot(jnp.concatenate([back_x, back_x], axis=1), ty[...].reshape(768, 256))
    for e in range(EXCITE):
        upper, lower = back[e * 128 : e * 128 + 64], back[e * 128 + 64 : (e + 1) * 128]
        re = upper[:, :128] - lower[:, 128:]
        im = lower[:, :128] + upper[:, 128:]
        for xl in range(2):
            out[pl.ds(8 * xl + e, NTGT, stride=16), :] = re[xl * 32 : (xl + 1) * 32]
            out[pl.ds(8 * xl + 4 + e, NTGT, stride=16), :] = im[xl * 32 : (xl + 1) * 32]
    send2[...] = out[:512, :].astype(jnp.bfloat16).reshape(NTGT, 16, 128)

    for dy, dz in FAR_FIRST:
        to = lax.rem(y + dy, NY) * NZ + lax.rem(z + dz + 1 + z_lo, NZ)
        pltpu.make_async_remote_copy(
            src_ref=send2.at[to],
            dst_ref=recv2.at[t],
            send_sem=send_sem2,
            recv_sem=recv_sem2,
            device_id={"tgt": to, "src": served},
            device_id_type=MESH,
        ).start()
    pltpu.make_async_copy(recv2, recv2, recv_sem2).wait()

    both = []
    for p in range(NY):
        total = recv2[NZ * p].astype(jnp.float32)
        for k in range(1, NZ):
            total = total + recv2[NZ * p + k].astype(jnp.float32)
        both.append(jnp.concatenate([total[:8], total[8:]], axis=1))
    both = jnp.concatenate(both, axis=0)
    hi, lo = split_up(both)
    for comp in range(6):
        field = dot(hi, place[comp]) + dot(lo, place[comp])
        for w in range(WAVES):
            ar = alpha[2 * (comp // 3)][w : w + 1, :]
            ai = alpha[2 * (comp // 3) + 1][w : w + 1, :]
            fr = field[w * 16 : w * 16 + 4]
            fi = field[w * 16 + 4 : w * 16 + 8]
            gf_ref[w, 0, comp] = ar * fr - ai * fi
            gf_ref[w, 1, comp] = ar * fi + ai * fr
            ga_ref[w, 0, comp] = field[w * 16 + 8 : w * 16 + 12]
            ga_ref[w, 1, comp] = field[w * 16 + 12 : w * 16 + 16]

    for _ in range(3):
        pltpu.make_async_copy(send1, send1, send_sem1).wait()
    pltpu.make_async_copy(send2, send2, send_sem2).wait()


def per_device(lattice, material, polarizability, wavenumber, dipoles, adjoint_in):
    f32, bf16 = jnp.float32, jnp.bfloat16
    constants = [
        jnp.asarray(make())
        for make in (
            source_y_matrix, source_x_matrix, target_x_matrix, target_y_matrix, table_x_matrix, table_y_matrix,
        )
    ]
    operands = [
        lattice,
        material.reshape(1, ATOMS),
        jnp.transpose(polarizability, (0, 2, 1)),
        wavenumber,
        dipoles,
        adjoint_in,
        *constants,
    ]
    field_shape = jax.ShapeDtypeStruct(dipoles.shape, f32)
    staged = [
        pltpu.SMEM(v.shape, v.dtype) if n == 3 else pltpu.VMEM(v.shape[1:] if n == 7 else v.shape, v.dtype)
        for n, v in enumerate(operands)
    ]
    from_forward, from_adjoint = pl.pallas_call(
        kernel,
        out_shape=(field_shape, field_shape),
        in_specs=[pl.BlockSpec(memory_space=pltpu.HBM)] * len(operands),
        out_specs=(pl.BlockSpec(memory_space=pltpu.VMEM),) * 2,
        scratch_shapes=staged
        + [
            pltpu.VMEM((6, 64, ATOMS), f32),
            pltpu.VMEM((NY, 16, 128), bf16),
            pltpu.VMEM((3 * NY, 16, 128), bf16),
            pltpu.VMEM((6, 136, 128), f32),
            pltpu.VMEM((12, KX, 128), f32),
            pltpu.VMEM((EXCITE, KX, 768), f32),
            pltpu.VMEM((EXCITE, KX, 768), bf16),
            pltpu.VMEM((528, 128), f32),
            pltpu.VMEM((NTGT, 16, 128), bf16),
            pltpu.VMEM((NTGT, 16, 128), bf16),
            pltpu.VMEM((6, 256, ATOMS), bf16),
            pltpu.SemaphoreType.DMA((12,)),
            pltpu.SemaphoreType.DMA,
            pltpu.SemaphoreType.DMA,
            pltpu.SemaphoreType.DMA,
            pltpu.SemaphoreType.DMA,
        ],
        compiler_params=pltpu.CompilerParams(
            collective_id=0, has_side_effects=True, vmem_limit_bytes=40 * 1024 * 1024
        ),
    )(*[pltpu.with_memory_space_constraint(v, pltpu.HBM) for v in operands])
    forward_out = dipoles.astype(f32) - from_forward
    adjoint_out = adjoint_in.astype(f32) - from_adjoint
    return forward_out, adjoint_out


def solution(mesh):
    spec = P(None, None, None, None, ("tgt", "src"))
    in_specs = (P(None, ("tgt", "src")), P(("tgt", "src")), P(), P(), spec, spec)
    return jax.shard_map(
        per_device, mesh=mesh, in_specs=in_specs, out_specs=(spec, spec), check_vma=False
    )
```

```python
import functools

import jax
import jax.numpy as jnp
import ml_dtypes
import numpy as np
from jax import lax
from jax.experimental import pallas as pl
from jax.experimental.pallas import tpu as pltpu
from jax.sharding import PartitionSpec as P

MESH = pl.DeviceIdType.MESH
WAVES, EXCITE, TYPES, ATOMS = 4, 4, 16, 32
NY, NZ, NCOL, NTGT = 8, 4, 16, 32
KX, KY = 128, 64
RING = (4, 3, 5, 2, 6, 1, 7, 0)
FAR_FIRST = sorted(
    ((dy, dz) for dy in range(NY) for dz in range(NZ)),
    key=lambda o: -(min(o[0], NY - o[0]) + (3, 3, 1, 1)[o[1]]),
)


def halves(x):
    hi = x.astype(ml_dtypes.bfloat16)
    lo = (x - hi.astype(np.float64)).astype(ml_dtypes.bfloat16)
    return hi, lo


def source_y_matrix():
    out = np.zeros((3, 128, 2, 3, 2, KY))
    ky = np.arange(KY)
    for q in range(3):
        for comp in range(6):
            for y in range(16):
                angle = 2 * np.pi * ky * ((q - 1) * 16 + y) / KY
                out[q, comp * 16 + y, 0, comp % 3, comp // 3] = np.cos(angle)
                out[q, comp * 16 + y, 1, comp % 3, comp // 3] = -np.sin(angle)
    return np.stack(halves(out.reshape(384, 768)))


def rows_x(x):
    angle = 2 * np.pi * np.arange(64)[:, None] * x[None, :] / KX
    sine = np.sin(angle)
    sine[0] = np.cos(np.pi * x)
    return np.concatenate([np.cos(angle), sine], axis=0)


def source_x_matrix():
    ys, xl = np.meshgrid(np.arange(NY), np.arange(2), indexing="ij")
    per = []
    for z in range(NZ):
        value = rows_x((8 * ys + 2 * z + xl).reshape(-1))
        hi, lo = halves(np.concatenate([value, value], axis=1))
        per.append(np.concatenate([hi, lo, hi], axis=1))
    return np.stack(per)


def target_x_matrix():
    xs = (2 * np.arange(NTGT)[None, :] + np.arange(2)[:, None]).reshape(64)
    weight = np.full((KX, 1), 2.0)
    weight[0] = weight[64] = 1.0
    hi, lo = halves((weight * rows_x(xs)).T)
    return np.concatenate([hi, lo], axis=1)


def target_y_matrix():
    out = np.zeros((3, 2, KY, 2, 128))
    ky = np.arange(KY)
    for comp in range(6):
        for y in range(16):
            angle = 2 * np.pi * ky * y / KY
            out[comp % 3, comp // 3, :, 0, comp * 16 + y] = np.cos(angle)
            out[comp % 3, comp // 3, :, 1, comp * 16 + y] = np.sin(angle)
    return np.stack(halves(out.reshape(384, 256) / (KX * KY)))


def table_x_matrix():
    even = rows_x(np.arange(64)) * np.where(np.arange(64) == 0, 1.0, 2.0)
    odd = 2.0 * rows_x(np.arange(64))
    even[65:] = even[1:64]
    odd[64] = 0.0
    odd[:64] = odd[64:]
    return np.stack([np.concatenate(halves(m), axis=1) for m in (even, odd)])


def table_y_matrix():
    angle = 2 * np.pi * np.arange(KY)[None, :] * np.arange(32)[:, None] / KY
    cos = np.cos(angle) * np.where(np.arange(32) == 0, 1.0, 2.0)[:, None]
    sin = 2.0 * np.sin(angle)
    even = np.concatenate([cos, cos], axis=1)
    odd = np.concatenate([sin, sin], axis=1)
    even_signed = np.concatenate([cos, -cos], axis=1)
    odd_signed = np.concatenate([sin, -sin], axis=1)
    groups = (
        ((0, 0, even), (1, 1, even), (2, 2, even), (3, 3, even)),
        ((0, 0, even), (1, 1, even), (3, 2, odd_signed), (2, 3, -odd_signed)),
        ((1, 0, odd), (0, 1, -odd), (2, 2, even_signed), (3, 3, even_signed)),
    )
    out = []
    for group in groups:
        full = np.zeros((4, 32, 4, 128))
        for array, table, matrix in group:
            full[array, :, table, :] = matrix
        hi, lo = halves(full.reshape(128, 512))
        out.append(np.concatenate([hi, lo, hi], axis=0))
    return np.stack(out)


K0, KAA, KBB, KYS, KXYT, KXS = 0, 2, 4, 6, 8, 10


def split_up(x):
    hi = x.astype(jnp.bfloat16)
    lo = (x - hi.astype(jnp.float32)).astype(jnp.bfloat16)
    return hi, lo


def dot(a, b):
    return jnp.dot(a, b, preferred_element_type=jnp.float32)


def build_tables(wave, sigma, cx, cy, tables):
    lane = lax.broadcasted_iota(jnp.int32, (64, 128), 1)
    dx = lax.broadcasted_iota(jnp.int32, (64, 128), 0).astype(jnp.float32)
    dy = (lane % 32).astype(jnp.float32)
    quarter = lane // 32
    radius_sq = dx * dx + dy * dy
    present = radius_sq > 0.5
    radius = jnp.sqrt(jnp.where(present, radius_sq, 1.0))
    unit_x = dx / radius
    unit_y = dy / radius
    phase = wave * radius
    inverse = 1.0 / phase
    weight = jnp.where(present, inverse, 0.0)
    green_re = jnp.cos(phase) * weight
    green_im = jnp.sin(phase) * weight
    inv_sq = inverse * inverse
    near_re = green_re * (1.0 - inv_sq) - green_im * inverse
    near_im = green_im * (1.0 - inv_sq) + green_re * inverse
    long_re = green_re * (3.0 * inv_sq - 1.0) + 3.0 * green_im * inverse
    long_im = green_im * (3.0 * inv_sq - 1.0) - 3.0 * green_re * inverse
    cross_re = green_re - green_im * inverse
    cross_im = green_im + green_re * inverse

    def group(a, b, c, d):
        return jnp.where(
            quarter == 0, a, jnp.where(quarter == 1, b, jnp.where(quarter == 2, c, d))
        ).astype(jnp.bfloat16)

    xx, yy, xy = unit_x * unit_x, unit_y * unit_y, unit_x * unit_y
    groups = (
        (
            0,
            group(
                near_re,
                sigma * near_im,
                near_re + long_re * xx,
                sigma * (near_im + long_im * xx),
            ),
        ),
        (
            0,
            group(
                near_re + long_re * yy,
                sigma * (near_im + long_im * yy),
                sigma * (cross_re * unit_y),
                cross_im * unit_y,
            ),
        ),
        (
            1,
            group(
                long_re * xy,
                sigma * (long_im * xy),
                sigma * (cross_re * unit_x),
                cross_im * unit_x,
            ),
        ),
    )
    for n, (parity, values) in enumerate(groups):
        along_x = dot(cx[parity], jnp.concatenate([values, values], axis=0))
        hi, lo = split_up(along_x)
        full = dot(jnp.concatenate([hi, hi, lo], axis=1), cy[n])
        for k in range(4):
            tables[4 * n + k] = full[:, k * 128 : (k + 1) * 128]


def pointwise(xa, z_ref, tables):
    rows = 16

    def body(i, carry):
        at = pl.multiple_of(i * rows, rows)
        top, low = pl.ds(at, rows), pl.ds(at + 64, rows)
        even_top = {k: (tables[k, top, :], tables[k + 1, top, :]) for k in (K0, KAA, KBB, KYS)}
        even_low = {k: (tables[k, low, :], tables[k + 1, low, :]) for k in (K0, KAA, KBB, KYS)}
        odd = {k: (tables[k, top, :], tables[k + 1, top, :]) for k in (KXYT, KXS)}
        for e in range(EXCITE):

            def part(rows_of, j):
                return tuple(
                    xa[e, rows_of, c * 384 + j * 128 : c * 384 + (j + 1) * 128] for c in range(2)
                )

            cos = [part(top, j) for j in range(3)]
            sin = [part(low, j) for j in range(3)]
            cos_swapped = [(pltpu.roll(a, 64, 1), pltpu.roll(b, 64, 1)) for a, b in cos]
            sin_swapped = [(pltpu.roll(a, 64, 1), pltpu.roll(b, 64, 1)) for a, b in sin]

            def combine(terms):
                re = im = None
                for sign, (kr, ki), (vr, vi) in terms:
                    tr, ti = kr * vr - ki * vi, kr * vi + ki * vr
                    if re is None:
                        re, im = tr, ti
                    elif sign > 0:
                        re, im = re + tr, im + ti
                    else:
                        re, im = re - tr, im - ti
                return re, im

            for rows_of, even, own, own_sw, cross, cross_sw, s in (
                (top, even_top, cos, cos_swapped, sin, sin_swapped, -1),
                (low, even_low, sin, sin_swapped, cos, cos_swapped, 1),
            ):
                sums = (
                    ((1, even[KAA], own[0]), (s, odd[KXYT], cross[1]), (1, even[KYS], own_sw[2])),
                    ((1, even[KBB], own[1]), (s, odd[KXYT], cross[0]), (-s, odd[KXS], cross_sw[2])),
                    ((1, even[K0], own[2]), (s, odd[KXS], cross_sw[1]), (-1, even[KYS], own_sw[0])),
                )
                for j, terms in enumerate(sums):
                    for c, value in enumerate(combine(terms)):
                        z_ref[e, rows_of, c * 384 + j * 128 : c * 384 + (j + 1) * 128] = (
                            value.astype(jnp.bfloat16)
                        )
        return carry

    lax.fori_loop(0, 64 // rows, body, 0, unroll=4)


def kernel(
    lat_h, mat_h, pol_h, wn_h, dip_h, adj_h, by_h, bx_h, tx_h, ty_h, cx_h, cy_h,
    gf_ref, ga_ref,
    lat, mat, pol, wn, dip, adj, by, bx, tx, ty, cx, cy,
    vec, send1, recv1, xb, tables, xa, z_ref, out, send2, recv2, place,
    in_sem, send_sem1, recv_sem1, send_sem2, recv_sem2,
):
    t = lax.axis_index("tgt")
    col = lax.axis_index("src")
    y, z = t // NZ, lax.rem(t, NZ)
    z_lo = lax.rem(col // 2, 2)

    def other(b):
        return b + 2 - 4 * lax.rem(b // 2, 2)

    def around(b):
        return [lax.rem(b + NCOL - 1, NCOL), b, lax.rem(b + 1, NCOL)]

    served = other(col)
    sources = around(served)
    helpers = [other(b) for b in around(col)]

    barrier = pltpu.get_barrier_semaphore()
    for step in RING:
        peer = lax.rem(y + step, NY) * NZ + z
        for q in (0, 2, 1):
            pl.semaphore_signal(
                barrier, inc=1, device_id={"tgt": peer, "src": sources[q]}, device_id_type=MESH
            )
    for step in (2, 1, 3):
        pl.semaphore_signal(
            barrier, inc=1, device_id={"tgt": y * NZ + lax.rem(z + step, NZ)}, device_id_type=MESH
        )

    loads = [
        pltpu.make_async_copy(src, dst, in_sem.at[n])
        for n, (src, dst) in enumerate(
            (
                (lat_h, lat),
                (mat_h, mat),
                (pol_h, pol),
                (wn_h, wn),
                (dip_h, dip),
                (adj_h, adj),
                (cx_h, cx),
                (cy_h, cy),
                (by_h, by),
                (bx_h.at[z], bx),
                (tx_h, tx),
                (ty_h, ty),
            )
        )
    ]
    for load in loads:
        load.start()
    for load in loads[:6]:
        load.wait()

    kinds = lax.broadcasted_iota(jnp.int32, (TYPES, ATOMS), 0)
    onehot = (kinds == mat[...]).astype(jnp.float32)
    alpha = [
        jnp.dot(pol[k], onehot, precision=lax.Precision.HIGHEST, preferred_element_type=jnp.float32)
        for k in range(4)
    ]

    site = (lat[0:1, :] - 2 * t) * 16 + (lat[1:2, :] - 16 * col)
    row = lax.broadcasted_iota(jnp.int32, (256, ATOMS), 0)
    same = (row // 128) * 16 + row % 16 == site
    owner = (row % 128) // 16
    for comp in range(6):
        place[comp] = (same & (owner == comp)).astype(jnp.bfloat16)

    for w in range(WAVES):
        for comp in range(6):
            ar = alpha[2 * (comp // 3)][w : w + 1, :]
            ai = alpha[2 * (comp // 3) + 1][w : w + 1, :]
            vr = adj[w, 0, comp].astype(jnp.float32)
            vi = adj[w, 1, comp].astype(jnp.float32)
            vec[comp, w * 16 : w * 16 + 4, :] = dip[w, 0, comp].astype(jnp.float32)
            vec[comp, w * 16 + 4 : w * 16 + 8, :] = dip[w, 1, comp].astype(jnp.float32)
            vec[comp, w * 16 + 8 : w * 16 + 12, :] = ar * vr + ai * vi
            vec[comp, w * 16 + 12 : w * 16 + 16, :] = ar * vi - ai * vr
    placed = None
    for comp in range(6):
        term = lax.dot_general(
            vec[comp].astype(jnp.bfloat16),
            place[comp],
            (((1,), (1,)), ((), ())),
            preferred_element_type=jnp.float32,
        )
        placed = term if placed is None else placed + term
    for p in range(NY):
        part = placed[p * 8 : (p + 1) * 8]
        send1[p] = jnp.concatenate([part[:, :128], part[:, 128:]], axis=0).astype(jnp.bfloat16)

    pl.semaphore_wait(barrier, NZ - 1 + 3 * NY)

    for step in RING:
        to = lax.rem(y + step, NY)
        for q in (0, 2, 1):
            pltpu.make_async_remote_copy(
                src_ref=send1.at[to],
                dst_ref=recv1.at[(2 - q) * NY + y],
                send_sem=send_sem1,
                recv_sem=recv_sem1,
                device_id={"tgt": to * NZ + z, "src": helpers[q]},
                device_id_type=MESH,
            ).start()

    for load in loads[6:]:
        load.wait()
    wave = wn[y // 2]
    sigma = (1 - 2 * lax.rem(y, 2)).astype(jnp.float32)
    build_tables(wave, sigma, cx, cy, tables)

    pltpu.make_async_copy(recv1, recv1, recv_sem1).wait()

    arrived = jnp.concatenate(
        [recv1[q * NY : (q + 1) * NY].reshape(128, 128) for q in range(3)], axis=1
    )
    along_y = dot(jnp.concatenate([arrived, arrived], axis=1), by[...].reshape(768, 768))
    for n in range(6):
        xb[n, :128, :] = along_y[:, n * 128 : (n + 1) * 128]
    for e in range(EXCITE):
        sums = [
            [
                jnp.concatenate(
                    [xb[3 * g + j, pl.ds(4 * ri + e, 16, stride=8), :] for j in range(3)], axis=1
                )
                for ri in range(2)
            ]
            for g in range(2)
        ]
        real = jnp.concatenate([sums[0][0], -sums[1][1]], axis=0)
        imag = jnp.concatenate([sums[0][1], sums[1][0]], axis=0)
        hi, lo = split_up(jnp.concatenate([real, imag], axis=1))
        xa[e] = dot(bx[...], jnp.concatenate([hi, hi, lo], axis=0))
    pointwise(xa, z_ref, tables)
    back_x = []
    for e in range(EXCITE):
        value = z_ref[e]
        along = dot(tx[...], jnp.concatenate([value, value], axis=0)).astype(jnp.bfloat16)
        back_x.append(jnp.concatenate([along[:, :384], along[:, 384:]], axis=0))
    back_x = jnp.concatenate(back_x, axis=0)
    back = dot(jnp.concatenate([back_x, back_x], axis=1), ty[...].reshape(768, 256))
    for e in range(EXCITE):
        upper, lower = back[e * 128 : e * 128 + 64], back[e * 128 + 64 : (e + 1) * 128]
        re = upper[:, :128] - lower[:, 128:]
        im = lower[:, :128] + upper[:, 128:]
        for xl in range(2):
            out[pl.ds(8 * xl + e, NTGT, stride=16), :] = re[xl * 32 : (xl + 1) * 32]
            out[pl.ds(8 * xl + 4 + e, NTGT, stride=16), :] = im[xl * 32 : (xl + 1) * 32]
    send2[...] = out[:512, :].astype(jnp.bfloat16).reshape(NTGT, 16, 128)

    for dy, dz in FAR_FIRST:
        to = lax.rem(y + dy, NY) * NZ + lax.rem(z + dz + 1 + z_lo, NZ)
        pltpu.make_async_remote_copy(
            src_ref=send2.at[to],
            dst_ref=recv2.at[z * NY + y],
            send_sem=send_sem2,
            recv_sem=recv_sem2.at[z],
            device_id={"tgt": to, "src": served},
            device_id_type=MESH,
        ).start()
    fields = [None] * 6
    for k in range(NZ):
        blocks = recv2.at[pl.ds(k * NY, NY)]
        pltpu.make_async_copy(blocks, blocks, recv_sem2.at[k]).wait()
        both = []
        for p in range(NY):
            part = recv2[k * NY + p].astype(jnp.float32)
            both.append(jnp.concatenate([part[:8], part[8:]], axis=1))
        both = jnp.concatenate(both, axis=0).astype(jnp.bfloat16)
        for comp in range(6):
            term = dot(both, place[comp])
            fields[comp] = term if k == 0 else fields[comp] + term
    for comp in range(6):
        field = fields[comp]
        for w in range(WAVES):
            ar = alpha[2 * (comp // 3)][w : w + 1, :]
            ai = alpha[2 * (comp // 3) + 1][w : w + 1, :]
            fr = field[w * 16 : w * 16 + 4]
            fi = field[w * 16 + 4 : w * 16 + 8]
            gf_ref[w, 0, comp] = ar * fr - ai * fi
            gf_ref[w, 1, comp] = ar * fi + ai * fr
            ga_ref[w, 0, comp] = field[w * 16 + 8 : w * 16 + 12]
            ga_ref[w, 1, comp] = field[w * 16 + 12 : w * 16 + 16]

    for _ in range(3):
        pltpu.make_async_copy(send1, send1, send_sem1).wait()
    pltpu.make_async_copy(send2, send2, send_sem2).wait()


def per_device(lattice, material, polarizability, wavenumber, dipoles, adjoint_in):
    f32, bf16 = jnp.float32, jnp.bfloat16
    constants = [
        jnp.asarray(make())
        for make in (
            source_y_matrix, source_x_matrix, target_x_matrix, target_y_matrix, table_x_matrix, table_y_matrix,
        )
    ]
    operands = [
        lattice,
        material.reshape(1, ATOMS),
        jnp.transpose(polarizability, (0, 2, 1)),
        wavenumber,
        dipoles,
        adjoint_in,
        *constants,
    ]
    field_shape = jax.ShapeDtypeStruct(dipoles.shape, f32)
    staged = [
        pltpu.SMEM(v.shape, v.dtype) if n == 3 else pltpu.VMEM(v.shape[1:] if n == 7 else v.shape, v.dtype)
        for n, v in enumerate(operands)
    ]
    from_forward, from_adjoint = pl.pallas_call(
        kernel,
        out_shape=(field_shape, field_shape),
        in_specs=[pl.BlockSpec(memory_space=pltpu.HBM)] * len(operands),
        out_specs=(pl.BlockSpec(memory_space=pltpu.VMEM),) * 2,
        scratch_shapes=staged
        + [
            pltpu.VMEM((6, 64, ATOMS), f32),
            pltpu.VMEM((NY, 16, 128), bf16),
            pltpu.VMEM((3 * NY, 16, 128), bf16),
            pltpu.VMEM((6, 136, 128), f32),
            pltpu.VMEM((12, KX, 128), f32),
            pltpu.VMEM((EXCITE, KX, 768), f32),
            pltpu.VMEM((EXCITE, KX, 768), bf16),
            pltpu.VMEM((528, 128), f32),
            pltpu.VMEM((NTGT, 16, 128), bf16),
            pltpu.VMEM((NTGT, 16, 128), bf16),
            pltpu.VMEM((6, 256, ATOMS), bf16),
            pltpu.SemaphoreType.DMA((12,)),
            pltpu.SemaphoreType.DMA,
            pltpu.SemaphoreType.DMA,
            pltpu.SemaphoreType.DMA,
            pltpu.SemaphoreType.DMA((NZ,)),
        ],
        compiler_params=pltpu.CompilerParams(
            collective_id=0, has_side_effects=True, vmem_limit_bytes=40 * 1024 * 1024
        ),
    )(*[pltpu.with_memory_space_constraint(v, pltpu.HBM) for v in operands])
    forward_out = dipoles.astype(f32) - from_forward
    adjoint_out = adjoint_in.astype(f32) - from_adjoint
    return forward_out, adjoint_out


def solution(mesh):
    spec = P(None, None, None, None, ("tgt", "src"))
    in_specs = (P(None, ("tgt", "src")), P(("tgt", "src")), P(), P(), spec, spec)
    return jax.shard_map(
        per_device, mesh=mesh, in_specs=in_specs, out_specs=(spec, spec), check_vma=False
    )
```

```python
import functools

import jax
import jax.numpy as jnp
import ml_dtypes
import numpy as np
from jax import lax
from jax.experimental import pallas as pl
from jax.experimental.pallas import tpu as pltpu
from jax.sharding import PartitionSpec as P

MESH = pl.DeviceIdType.MESH
WAVES, EXCITE, TYPES, ATOMS = 4, 4, 16, 32
NY, NZ, NCOL, NTGT = 8, 4, 16, 32
KX, KY = 128, 64
RING = (4, 3, 5, 2, 6, 1, 7, 0)
FAR_FIRST = sorted(
    ((dy, dz) for dy in range(NY) for dz in range(NZ)),
    key=lambda o: -(min(o[0], NY - o[0]) + (3, 3, 1, 1)[o[1]]),
)


def halves(x):
    hi = x.astype(ml_dtypes.bfloat16)
    lo = (x - hi.astype(np.float64)).astype(ml_dtypes.bfloat16)
    return hi, lo


def source_y_matrix():
    out = np.zeros((3, 128, 2, 3, 2, KY))
    ky = np.arange(KY)
    for q in range(3):
        for comp in range(6):
            for y in range(16):
                angle = 2 * np.pi * ky * ((q - 1) * 16 + y) / KY
                out[q, comp * 16 + y, 0, comp % 3, comp // 3] = np.cos(angle)
                out[q, comp * 16 + y, 1, comp % 3, comp // 3] = -np.sin(angle)
    return np.stack(halves(out.reshape(384, 768)))


def rows_x(x):
    angle = 2 * np.pi * np.arange(64)[:, None] * x[None, :] / KX
    sine = np.sin(angle)
    sine[0] = np.cos(np.pi * x)
    return np.concatenate([np.cos(angle), sine], axis=0)


def source_x_matrix():
    ys, xl = np.meshgrid(np.arange(NY), np.arange(2), indexing="ij")
    per = []
    for z in range(NZ):
        value = rows_x((8 * ys + 2 * z + xl).reshape(-1))
        hi, lo = halves(np.concatenate([value, value], axis=1))
        per.append(np.concatenate([hi, lo, hi], axis=1))
    return np.stack(per)


def target_x_matrix():
    xs = (2 * np.arange(NTGT)[None, :] + np.arange(2)[:, None]).reshape(64)
    weight = np.full((KX, 1), 2.0)
    weight[0] = weight[64] = 1.0
    hi, lo = halves((weight * rows_x(xs)).T)
    return np.concatenate([hi, lo], axis=1)


def target_y_matrix():
    out = np.zeros((3, 2, KY, 2, 128))
    ky = np.arange(KY)
    for comp in range(6):
        for y in range(16):
            angle = 2 * np.pi * ky * y / KY
            out[comp % 3, comp // 3, :, 0, comp * 16 + y] = np.cos(angle)
            out[comp % 3, comp // 3, :, 1, comp * 16 + y] = np.sin(angle)
    return np.stack(halves(out.reshape(384, 256) / (KX * KY)))


def table_x_matrix():
    even = rows_x(np.arange(64)) * np.where(np.arange(64) == 0, 1.0, 2.0)
    odd = 2.0 * rows_x(np.arange(64))
    even[65:] = even[1:64]
    odd[64] = 0.0
    odd[:64] = odd[64:]
    return np.stack([np.concatenate(halves(m), axis=1) for m in (even, odd)])


def table_y_matrix():
    angle = 2 * np.pi * np.arange(KY)[None, :] * np.arange(32)[:, None] / KY
    cos = np.cos(angle) * np.where(np.arange(32) == 0, 1.0, 2.0)[:, None]
    sin = 2.0 * np.sin(angle)
    even = np.concatenate([cos, cos], axis=1)
    odd = np.concatenate([sin, sin], axis=1)
    even_signed = np.concatenate([cos, -cos], axis=1)
    odd_signed = np.concatenate([sin, -sin], axis=1)
    groups = (
        ((0, 0, even), (1, 1, even), (2, 2, even), (3, 3, even)),
        ((0, 0, even), (1, 1, even), (3, 2, odd_signed), (2, 3, -odd_signed)),
        ((1, 0, odd), (0, 1, -odd), (2, 2, even_signed), (3, 3, even_signed)),
    )
    out = []
    for group in groups:
        full = np.zeros((4, 32, 4, 128))
        for array, table, matrix in group:
            full[array, :, table, :] = matrix
        hi, lo = halves(full.reshape(128, 512))
        out.append(np.concatenate([hi, lo, hi], axis=0))
    return np.stack(out)


K0, KAA, KBB, KYS, KXYT, KXS = 0, 2, 4, 6, 8, 10


def split_up(x):
    hi = x.astype(jnp.bfloat16)
    lo = (x - hi.astype(jnp.float32)).astype(jnp.bfloat16)
    return hi, lo


def dot(a, b):
    return jnp.dot(a, b, preferred_element_type=jnp.float32)


def build_tables(wave, sigma, cx, cy, tables):
    lane = lax.broadcasted_iota(jnp.int32, (64, 128), 1)
    dx = lax.broadcasted_iota(jnp.int32, (64, 128), 0).astype(jnp.float32)
    dy = (lane % 32).astype(jnp.float32)
    quarter = lane // 32
    radius_sq = dx * dx + dy * dy
    present = radius_sq > 0.5
    radius = jnp.sqrt(jnp.where(present, radius_sq, 1.0))
    unit_x = dx / radius
    unit_y = dy / radius
    phase = wave * radius
    inverse = 1.0 / phase
    weight = jnp.where(present, inverse, 0.0)
    green_re = jnp.cos(phase) * weight
    green_im = jnp.sin(phase) * weight
    inv_sq = inverse * inverse
    near_re = green_re * (1.0 - inv_sq) - green_im * inverse
    near_im = green_im * (1.0 - inv_sq) + green_re * inverse
    long_re = green_re * (3.0 * inv_sq - 1.0) + 3.0 * green_im * inverse
    long_im = green_im * (3.0 * inv_sq - 1.0) - 3.0 * green_re * inverse
    cross_re = green_re - green_im * inverse
    cross_im = green_im + green_re * inverse

    def group(a, b, c, d):
        return jnp.where(
            quarter == 0, a, jnp.where(quarter == 1, b, jnp.where(quarter == 2, c, d))
        ).astype(jnp.bfloat16)

    xx, yy, xy = unit_x * unit_x, unit_y * unit_y, unit_x * unit_y
    groups = (
        (
            0,
            group(
                near_re,
                sigma * near_im,
                near_re + long_re * xx,
                sigma * (near_im + long_im * xx),
            ),
        ),
        (
            0,
            group(
                near_re + long_re * yy,
                sigma * (near_im + long_im * yy),
                sigma * (cross_re * unit_y),
                cross_im * unit_y,
            ),
        ),
        (
            1,
            group(
                long_re * xy,
                sigma * (long_im * xy),
                sigma * (cross_re * unit_x),
                cross_im * unit_x,
            ),
        ),
    )
    for n, (parity, values) in enumerate(groups):
        along_x = dot(cx[parity], jnp.concatenate([values, values], axis=0))
        hi, lo = split_up(along_x)
        full = dot(jnp.concatenate([hi, hi, lo], axis=1), cy[n])
        for k in range(4):
            tables[4 * n + k] = full[:, k * 128 : (k + 1) * 128]


def pointwise(xa, z_ref, tables):
    rows = 16

    def body(i, carry):
        at = pl.multiple_of(i * rows, rows)
        top, low = pl.ds(at, rows), pl.ds(at + 64, rows)
        even_top = {k: (tables[k, top, :], tables[k + 1, top, :]) for k in (K0, KAA, KBB, KYS)}
        even_low = {k: (tables[k, low, :], tables[k + 1, low, :]) for k in (K0, KAA, KBB, KYS)}
        odd = {k: (tables[k, top, :], tables[k + 1, top, :]) for k in (KXYT, KXS)}
        for e in range(EXCITE):

            def part(rows_of, j):
                return tuple(
                    xa[e, rows_of, c * 384 + j * 128 : c * 384 + (j + 1) * 128] for c in range(2)
                )

            cos = [part(top, j) for j in range(3)]
            sin = [part(low, j) for j in range(3)]
            cos_swapped = [(pltpu.roll(a, 64, 1), pltpu.roll(b, 64, 1)) for a, b in cos]
            sin_swapped = [(pltpu.roll(a, 64, 1), pltpu.roll(b, 64, 1)) for a, b in sin]

            def combine(terms):
                re = im = None
                for sign, (kr, ki), (vr, vi) in terms:
                    tr, ti = kr * vr - ki * vi, kr * vi + ki * vr
                    if re is None:
                        re, im = tr, ti
                    elif sign > 0:
                        re, im = re + tr, im + ti
                    else:
                        re, im = re - tr, im - ti
                return re, im

            for rows_of, even, own, own_sw, cross, cross_sw, s in (
                (top, even_top, cos, cos_swapped, sin, sin_swapped, -1),
                (low, even_low, sin, sin_swapped, cos, cos_swapped, 1),
            ):
                sums = (
                    ((1, even[KAA], own[0]), (s, odd[KXYT], cross[1]), (1, even[KYS], own_sw[2])),
                    ((1, even[KBB], own[1]), (s, odd[KXYT], cross[0]), (-s, odd[KXS], cross_sw[2])),
                    ((1, even[K0], own[2]), (s, odd[KXS], cross_sw[1]), (-1, even[KYS], own_sw[0])),
                )
                for j, terms in enumerate(sums):
                    for c, value in enumerate(combine(terms)):
                        z_ref[e, rows_of, c * 384 + j * 128 : c * 384 + (j + 1) * 128] = (
                            value.astype(jnp.bfloat16)
                        )
        return carry

    lax.fori_loop(0, 64 // rows, body, 0, unroll=4)


def kernel(
    lat_h, mat_h, pol_h, wn_h, dip_h, adj_h, by_h, bx_h, tx_h, ty_h, cx_h, cy_h,
    gf_ref, ga_ref,
    lat, mat, pol, wn, dip, adj, by, bx, tx, ty, cx, cy,
    vec, send1, recv1, xb, tables, xa, z_ref, out, send2, recv2, place,
    in_sem, send_sem1, recv_sem1, send_sem2, recv_sem2,
):
    t = lax.axis_index("tgt")
    col = lax.axis_index("src")
    y, z = t // NZ, lax.rem(t, NZ)
    z_lo = lax.rem(col // 2, 2)

    def other(b):
        return b + 2 - 4 * lax.rem(b // 2, 2)

    def around(b):
        return [lax.rem(b + NCOL - 1, NCOL), b, lax.rem(b + 1, NCOL)]

    served = other(col)
    sources = around(served)
    helpers = [other(b) for b in around(col)]

    barrier = pltpu.get_barrier_semaphore()
    for step in RING:
        peer = lax.rem(y + step, NY) * NZ + z
        for q in (0, 2, 1):
            pl.semaphore_signal(
                barrier, inc=1, device_id={"tgt": peer, "src": sources[q]}, device_id_type=MESH
            )
    for step in (2, 1, 3):
        pl.semaphore_signal(
            barrier, inc=1, device_id={"tgt": y * NZ + lax.rem(z + step, NZ)}, device_id_type=MESH
        )

    loads = [
        pltpu.make_async_copy(src, dst, in_sem.at[n])
        for n, (src, dst) in enumerate(
            (
                (lat_h, lat),
                (mat_h, mat),
                (pol_h, pol),
                (wn_h, wn),
                (dip_h, dip),
                (adj_h, adj),
                (cx_h, cx),
                (cy_h, cy),
                (by_h, by),
                (bx_h.at[z], bx),
                (tx_h, tx),
                (ty_h, ty),
            )
        )
    ]
    for load in loads:
        load.start()
    for load in loads[:6]:
        load.wait()

    kinds = lax.broadcasted_iota(jnp.int32, (TYPES, ATOMS), 0)
    onehot = (kinds == mat[...]).astype(jnp.float32)
    alpha = [
        jnp.dot(pol[k], onehot, precision=lax.Precision.HIGHEST, preferred_element_type=jnp.float32)
        for k in range(4)
    ]

    site = (lat[0:1, :] - 2 * t) * 16 + (lat[1:2, :] - 16 * col)
    row = lax.broadcasted_iota(jnp.int32, (256, ATOMS), 0)
    same = (row // 128) * 16 + row % 16 == site
    owner = (row % 128) // 16
    for comp in range(6):
        place[comp] = (same & (owner == comp)).astype(jnp.bfloat16)

    for w in range(WAVES):
        for comp in range(6):
            ar = alpha[2 * (comp // 3)][w : w + 1, :]
            ai = alpha[2 * (comp // 3) + 1][w : w + 1, :]
            vr = adj[w, 0, comp].astype(jnp.float32)
            vi = adj[w, 1, comp].astype(jnp.float32)
            vec[comp, w * 16 : w * 16 + 4, :] = dip[w, 0, comp].astype(jnp.float32)
            vec[comp, w * 16 + 4 : w * 16 + 8, :] = dip[w, 1, comp].astype(jnp.float32)
            vec[comp, w * 16 + 8 : w * 16 + 12, :] = ar * vr + ai * vi
            vec[comp, w * 16 + 12 : w * 16 + 16, :] = ar * vi - ai * vr
    placed = None
    for comp in range(6):
        term = lax.dot_general(
            vec[comp].astype(jnp.bfloat16),
            place[comp],
            (((1,), (1,)), ((), ())),
            preferred_element_type=jnp.float32,
        )
        placed = term if placed is None else placed + term
    for p in range(NY):
        part = placed[p * 8 : (p + 1) * 8]
        send1[p] = jnp.concatenate([part[:, :128], part[:, 128:]], axis=0).astype(jnp.bfloat16)

    pl.semaphore_wait(barrier, NZ - 1 + 3 * NY)

    for step in RING:
        to = lax.rem(y + step, NY)
        for q in (0, 2, 1):
            pltpu.make_async_remote_copy(
                src_ref=send1.at[to],
                dst_ref=recv1.at[(2 - q) * NY + y],
                send_sem=send_sem1,
                recv_sem=recv_sem1,
                device_id={"tgt": to * NZ + z, "src": helpers[q]},
                device_id_type=MESH,
            ).start()

    for load in loads[6:]:
        load.wait()
    wave = wn[y // 2]
    sigma = (1 - 2 * lax.rem(y, 2)).astype(jnp.float32)
    build_tables(wave, sigma, cx, cy, tables)

    pltpu.make_async_copy(recv1, recv1, recv_sem1).wait()

    arrived = jnp.concatenate(
        [recv1[q * NY : (q + 1) * NY].reshape(128, 128) for q in range(3)], axis=1
    )
    along_y = dot(jnp.concatenate([arrived, arrived], axis=1), by[...].reshape(768, 768))
    for n in range(6):
        xb[n, :128, :] = along_y[:, n * 128 : (n + 1) * 128]
    for e in range(EXCITE):
        sums = [
            [
                jnp.concatenate(
                    [xb[3 * g + j, pl.ds(4 * ri + e, 16, stride=8), :] for j in range(3)], axis=1
                )
                for ri in range(2)
            ]
            for g in range(2)
        ]
        real = jnp.concatenate([sums[0][0], -sums[1][1]], axis=0)
        imag = jnp.concatenate([sums[0][1], sums[1][0]], axis=0)
        hi, lo = split_up(jnp.concatenate([real, imag], axis=1))
        xa[e] = dot(bx[...], jnp.concatenate([hi, hi, lo], axis=0))
    pointwise(xa, z_ref, tables)
    for e in range(EXCITE):
        value = z_ref[e]
        along = dot(tx[...], jnp.concatenate([value, value], axis=0)).astype(jnp.bfloat16)
        along = jnp.concatenate([along[:, :384], along[:, 384:]], axis=0)
        back = dot(jnp.concatenate([along, along], axis=1), ty[...].reshape(768, 256))
        re = back[:64, :128] - back[64:, 128:]
        im = back[64:, :128] + back[:64, 128:]
        for xl in range(2):
            out[pl.ds(8 * xl + e, NTGT, stride=16), :] = re[xl * 32 : (xl + 1) * 32]
            out[pl.ds(8 * xl + 4 + e, NTGT, stride=16), :] = im[xl * 32 : (xl + 1) * 32]
    send2[...] = out[:512, :].astype(jnp.bfloat16).reshape(NTGT, 16, 128)

    for dy, dz in FAR_FIRST:
        to = lax.rem(y + dy, NY) * NZ + lax.rem(z + dz + 1 + z_lo, NZ)
        pltpu.make_async_remote_copy(
            src_ref=send2.at[to],
            dst_ref=recv2.at[z * NY + y],
            send_sem=send_sem2,
            recv_sem=recv_sem2.at[z],
            device_id={"tgt": to, "src": served},
            device_id_type=MESH,
        ).start()
    fields = [None] * 6
    for k in range(NZ):
        blocks = recv2.at[pl.ds(k * NY, NY)]
        pltpu.make_async_copy(blocks, blocks, recv_sem2.at[k]).wait()
        both = []
        for p in range(NY):
            part = recv2[k * NY + p].astype(jnp.float32)
            both.append(jnp.concatenate([part[:8], part[8:]], axis=1))
        both = jnp.concatenate(both, axis=0).astype(jnp.bfloat16)
        for comp in range(6):
            term = dot(both, place[comp])
            fields[comp] = term if k == 0 else fields[comp] + term
    for comp in range(6):
        field = fields[comp]
        for w in range(WAVES):
            ar = alpha[2 * (comp // 3)][w : w + 1, :]
            ai = alpha[2 * (comp // 3) + 1][w : w + 1, :]
            fr = field[w * 16 : w * 16 + 4]
            fi = field[w * 16 + 4 : w * 16 + 8]
            gf_ref[w, 0, comp] = ar * fr - ai * fi
            gf_ref[w, 1, comp] = ar * fi + ai * fr
            ga_ref[w, 0, comp] = field[w * 16 + 8 : w * 16 + 12]
            ga_ref[w, 1, comp] = field[w * 16 + 12 : w * 16 + 16]

    for _ in range(3):
        pltpu.make_async_copy(send1, send1, send_sem1).wait()
    pltpu.make_async_copy(send2, send2, send_sem2).wait()


def per_device(lattice, material, polarizability, wavenumber, dipoles, adjoint_in):
    f32, bf16 = jnp.float32, jnp.bfloat16
    constants = [
        jnp.asarray(make())
        for make in (
            source_y_matrix, source_x_matrix, target_x_matrix, target_y_matrix, table_x_matrix, table_y_matrix,
        )
    ]
    operands = [
        lattice,
        material.reshape(1, ATOMS),
        jnp.transpose(polarizability, (0, 2, 1)),
        wavenumber,
        dipoles,
        adjoint_in,
        *constants,
    ]
    field_shape = jax.ShapeDtypeStruct(dipoles.shape, f32)
    staged = [
        pltpu.SMEM(v.shape, v.dtype) if n == 3 else pltpu.VMEM(v.shape[1:] if n == 7 else v.shape, v.dtype)
        for n, v in enumerate(operands)
    ]
    from_forward, from_adjoint = pl.pallas_call(
        kernel,
        out_shape=(field_shape, field_shape),
        in_specs=[pl.BlockSpec(memory_space=pltpu.HBM)] * len(operands),
        out_specs=(pl.BlockSpec(memory_space=pltpu.VMEM),) * 2,
        scratch_shapes=staged
        + [
            pltpu.VMEM((6, 64, ATOMS), f32),
            pltpu.VMEM((NY, 16, 128), bf16),
            pltpu.VMEM((3 * NY, 16, 128), bf16),
            pltpu.VMEM((6, 136, 128), f32),
            pltpu.VMEM((12, KX, 128), f32),
            pltpu.VMEM((EXCITE, KX, 768), f32),
            pltpu.VMEM((EXCITE, KX, 768), bf16),
            pltpu.VMEM((528, 128), f32),
            pltpu.VMEM((NTGT, 16, 128), bf16),
            pltpu.VMEM((NTGT, 16, 128), bf16),
            pltpu.VMEM((6, 256, ATOMS), bf16),
            pltpu.SemaphoreType.DMA((12,)),
            pltpu.SemaphoreType.DMA,
            pltpu.SemaphoreType.DMA,
            pltpu.SemaphoreType.DMA,
            pltpu.SemaphoreType.DMA((NZ,)),
        ],
        compiler_params=pltpu.CompilerParams(
            collective_id=0, has_side_effects=True, vmem_limit_bytes=40 * 1024 * 1024
        ),
    )(*[pltpu.with_memory_space_constraint(v, pltpu.HBM) for v in operands])
    forward_out = dipoles.astype(f32) - from_forward
    adjoint_out = adjoint_in.astype(f32) - from_adjoint
    return forward_out, adjoint_out


def solution(mesh):
    spec = P(None, None, None, None, ("tgt", "src"))
    in_specs = (P(None, ("tgt", "src")), P(("tgt", "src")), P(), P(), spec, spec)
    return jax.shard_map(
        per_device, mesh=mesh, in_specs=in_specs, out_specs=(spec, spec), check_vma=False
    )
```
